512 devices in a mesh: replica: 16 (over x_lo, y, core), section: 16 (over z), tensor: 2 (over x_hi).
Axes of the slice: x: 4 (x_hi: 2, x_lo: 2; x = x_hi * 2 + x_lo), y: 4, z: 16, core: 2. Of those that a mesh axis runs over, the one named last changes fastest.
Arguments:
- cotangent: bfloat16 [16, 3, 64, 8192], P('replica', None, None, 'tensor'), may hold values from -4 to 4
- saved_pre: bfloat16 [16, 16, 3, 64, 64], P('replica', 'section'), may hold values from -6 to 6
- up_band: bfloat16 [16, 1024, 8192], P('replica', 'section', 'tensor'), may hold values from -0.75 to 0.75
- down_band: bfloat16 [16, 1024, 8192], P('replica', 'section', 'tensor'), may hold values from -0.03125 to 0.03125
- accumulated: float32 [16, 1024, 8192], P('replica', 'section', 'tensor'), may hold values from -8 to 8
- outer_momentum: float32 [16, 2, 64, 4096], P('section', 'tensor', None, 'replica'), may hold values from -0.6 to 0.6
- band_freqs: int32 [2, 8], replicated, may hold values from 0 to 15, as said below
- sync_flags: int32 [16], P('section'), may hold values from 0 to 1, as said below
Outputs:
- residual: float32 [16, 1024, 8192], P('replica', 'section', 'tensor')
- new_outer_momentum: float32 [16, 2, 64, 4096], P('section', 'tensor', None, 'replica')
- outer_step: float32 [16, 2, 64, 4096], P('section', 'tensor', None, 'replica')
The draws below stay inside these ranges and needn't reach their ends.
Inputs may be any that keep to these rules, and one draw needn't show every extreme that they name: `band_freqs`: each row holds 8 distinct frequencies, among them 0 and 15. `sync_flags`: exactly half of the sections have 1, the others 0.
All inputs are finite; a program needn't handle non-finite values.
Results may differ from the reference program's by a relative error of at most 0.019.
Values may be sent and summed in bfloat16 or wider, within the bound.
A program may use at most 64 MiB of HBM per device.

```python
import jax
import jax.numpy as jnp
from jax import lax

D = 8192
FF = 28672
BAND = 64
SPAN = 64
LOW = 8
TOK = 64
MB = 3
REPLICAS = 16
SECTIONS = 16
HALVES = 2
DH = 4096
ROWS = 1024


def draw_band_freqs(key, part):
    key = jax.random.fold_in(key, 11)
    freq_rows = []
    for which_row in range(2):
        row_key = jax.random.fold_in(key, which_row)
        shuffled = jax.random.permutation(row_key, 2 * LOW - 2).astype(jnp.int32) + 1
        freq_rows.append(jnp.concatenate([jnp.zeros((1,), jnp.int32), shuffled[:LOW - 2], jnp.full((1,), 2 * LOW - 1, jnp.int32)]))
    return jnp.stack(freq_rows)


def draw_sync_flags(key, part):
    key = jax.random.fold_in(key, 23)
    shuffled = jax.random.permutation(key, SECTIONS).astype(jnp.int32)
    return jnp.where(shuffled < SECTIONS // 2, 1, 0).astype(jnp.int32)


def shard_levels(key, dims, pieces, low, largest):
    level = 1.0
    for position, blocks in pieces:
        steps = jax.random.uniform(jax.random.fold_in(jax.random.fold_in(key, 6), position), (blocks,), jnp.float32, low / len(pieces), largest / len(pieces))
        level = level * jnp.repeat(jnp.exp(steps), dims[position] // blocks).reshape((-1,) + (1,) * (len(dims) - 1 - position))
    return level


def scatter_about(rng, dims, width, most, pieces=(), kind=jnp.bfloat16):
    gain = shard_levels(rng, dims, pieces, -0.22, 0.18) if pieces else 1.0
    entries = jax.random.normal(rng, dims, jnp.float32) * width * gain
    return jnp.minimum(jnp.maximum(entries, -most), most).astype(kind)


def setup_inputs(seed: int = 0) -> dict:
    key_of = jax.random.split(jax.random.key(seed), 9)
    cotangent = scatter_about(key_of[0], (REPLICAS, MB, TOK, D), 0.25, 4.0, ((0, 16), (3, 2)))
    saved_pre = scatter_about(key_of[1], (REPLICAS, SECTIONS, MB, TOK, BAND), 1.0, 6.0, ((0, 16), (1, 16)))
    up_band = scatter_about(key_of[2], (REPLICAS, ROWS, D), BAND ** -0.5, 0.75, ((0, 16), (1, 16), (2, 2)))
    down_band = scatter_about(key_of[3], (REPLICAS, ROWS, D), FF ** -0.5, 0.03125, ((0, 16), (1, 16), (2, 2)))
    accumulated = scatter_about(key_of[4], (REPLICAS, ROWS, D), 2.0, 8.0, ((0, 16), (1, 16), (2, 2)), jnp.float32)
    outer_momentum = scatter_about(key_of[5], (SECTIONS, HALVES, BAND, DH), 0.1, 0.6, ((0, 16), (1, 2), (3, 16)), jnp.float32)
    band_freqs = draw_band_freqs(jax.random.fold_in(key_of[8], 71), 0)
    sync_flags = draw_sync_flags(jax.random.fold_in(key_of[8], 71), 0)
    return dict(cotangent=cotangent, saved_pre=saved_pre, up_band=up_band, down_band=down_band, accumulated=accumulated, outer_momentum=outer_momentum, band_freqs=band_freqs, sync_flags=sync_flags)


momentum_decay = 0.9
outer_rate = 0.7

def silu_slope(values):
    sigma = jax.nn.sigmoid(values)
    return sigma * (1.0 + values * (1.0 - sigma))

def dct_rows(frequencies, length):
    positions = jnp.arange(length, dtype=jnp.float32) + 0.5
    angles = jnp.pi * frequencies.astype(jnp.float32)[:, None] * positions[None, :] / length
    weights = jnp.where(frequencies[:, None] == 0, jnp.sqrt(1.0 / length), jnp.sqrt(2.0 / length))
    return weights * jnp.cos(angles)

def reference(cotangent, saved_pre, up_band, down_band, accumulated, outer_momentum, band_freqs, sync_flags):
    highest = lax.Precision.HIGHEST
    grad_list = [jnp.zeros((REPLICAS, BAND, D), jnp.float32) for section_idx in range(SECTIONS)]
    for micro_idx in range(MB):
        incoming = cotangent[:, micro_idx]
        for section_idx in range(SECTIONS - 1, -1, -1):
            row_start = section_idx * BAND
            w_down = down_band[:, row_start:row_start + BAND].astype(jnp.float32)
            w_up = up_band[:, row_start:row_start + BAND].astype(jnp.float32)
            grad_out = incoming.astype(jnp.float32)
            pre_now = saved_pre[:, section_idx, micro_idx].astype(jnp.float32)
            hidden_grad = jnp.einsum('rtd,rhd->rth', grad_out, w_down, precision=highest)
            pre_grad = (hidden_grad * silu_slope(pre_now)).astype(jnp.bfloat16)
            hidden = jax.nn.silu(pre_now).astype(jnp.bfloat16)
            grad_list[section_idx] = grad_list[section_idx] + jnp.einsum('rth,rtd->rhd', hidden.astype(jnp.float32), grad_out, precision=highest)
            passed = grad_out + jnp.einsum('rth,rhd->rtd', pre_grad.astype(jnp.float32), w_up, precision=highest)
            incoming = passed.astype(jnp.bfloat16)
    row_basis = dct_rows(band_freqs[0], SPAN)
    col_basis = dct_rows(band_freqs[1], SPAN)
    groups = BAND // SPAN
    blocks = D // SPAN
    residual_parts = []
    moment_parts = []
    step_parts = []
    for section_idx in range(SECTIONS):
        row_start = section_idx * BAND
        moment = accumulated[:, row_start:row_start + BAND] + grad_list[section_idx]
        tile_view = moment.reshape(REPLICAS, groups, SPAN, blocks, SPAN)
        coeffs = jnp.einsum('ui,rgicj->rgucj', row_basis, tile_view, precision=highest)
        coeffs = jnp.einsum('rgucj,vj->rgucv', coeffs, col_basis, precision=highest)
        half_back = jnp.einsum('rgucv,vj->rgucj', coeffs, col_basis, precision=highest)
        decoded = jnp.einsum('ui,rgucj->rgicj', row_basis, half_back, precision=highest).reshape(REPLICAS, BAND, D)
        synced = sync_flags[section_idx] == 1
        residual_parts.append(jnp.where(synced, moment - decoded, moment))
        mean_coeffs = lax.optimization_barrier(jnp.sum(coeffs, axis=0)) / REPLICAS
        half_back = jnp.einsum('gucv,vj->gucj', mean_coeffs, col_basis, precision=highest)
        change = jnp.einsum('ui,gucj->gicj', row_basis, half_back, precision=highest).reshape(BAND, D)
        prior = jnp.transpose(outer_momentum[section_idx], (1, 0, 2)).reshape(BAND, D)
        new_moment = momentum_decay * prior + change
        stepped = -outer_rate * (change + momentum_decay * new_moment)
        moment_parts.append(jnp.where(synced, new_moment, prior))
        step_parts.append(jnp.where(synced, stepped, jnp.zeros_like(stepped)))
    residual = jnp.concatenate(residual_parts, axis=1)
    new_outer = jnp.transpose(jnp.stack(moment_parts).reshape(SECTIONS, BAND, HALVES, DH), (0, 2, 1, 3))
    outer_step = jnp.transpose(jnp.stack(step_parts).reshape(SECTIONS, BAND, HALVES, DH), (0, 2, 1, 3))
    return (residual, new_outer, outer_step)
```

```python
import math

import jax
import jax.numpy as jnp
from jax import lax
from jax.experimental import pallas as pl
from jax.experimental.pallas import tpu as pltpu
from jax.sharding import PartitionSpec as P

SPAN = 64
LOW = 8
momentum_decay = 0.9
outer_rate = 0.7

SECTIONS = 16
REPLICAS = 16
BAND = 64
COLS = 4096
ROWS = 192
CHUNK = 16
CHUNKS = ROWS // CHUNK
PIECES = 4
WIDTH = COLS // PIECES
MESH = pl.DeviceIdType.MESH
HIGH = lax.Precision.HIGHEST
BF = jnp.bfloat16
F32 = jnp.float32


def dot(a, b, precision=None):
    return jnp.dot(a, b, preferred_element_type=F32, precision=precision)


def dot_t(a, b, precision=None):
    return lax.dot_general(
        a, b, (((1,), (1,)), ((), ())), preferred_element_type=F32, precision=precision
    )


def basis(freqs, position):
    turns = (freqs * (2 * position + 1)) & (4 * SPAN - 1)
    weight = jnp.where(freqs == 0, math.sqrt(1.0 / SPAN), math.sqrt(2.0 / SPAN))
    return weight * jnp.cos(turns.astype(F32) * (math.pi / (2 * SPAN)))


def freqs_along(freq_ref, row, which):
    out = jnp.zeros_like(which)
    for k in range(LOW):
        out = jnp.where(which == k, freq_ref[row, k], out)
    return out


def kernel(
    freq_ref, flag_ref, cot_hbm, pre_ref, up_hbm, down_hbm, acc_hbm, outer_ref,
    res_ref, new_ref, step_ref,
    cot, wu, wd, acc, g, out, wd1, wd2, wu1, z, zsend, zbase, q, qsend, m1, m2, m1s, m2s, mcat,
    slope, hidden, coef, heard,
    load_sem, up1_s, up1_r, up2_s, up2_r, dn_s, dn_r, m1_s, m1_r, m2_s, m2_r, zb_s, zb_r,
    z_s, z_r, q_s, q_r, g_s, g_r, c_s, c_r,
):
    r = lax.axis_index("replica")
    s = lax.axis_index("section")
    t = lax.axis_index("tensor")
    other = 1 - t

    def sec(offset):
        return lax.rem(s + offset + SECTIONS, SECTIONS)

    def remote(src, dst, send, recv, section, tensor):
        return pltpu.make_async_remote_copy(
            src, dst, send, recv, device_id=(r, section, tensor), device_id_type=MESH
        )

    loads = [
        pltpu.make_async_copy(src, dst, load_sem.at[k])
        for k, (src, dst) in enumerate(
            ((down_hbm, wd), (cot_hbm, cot), (up_hbm, wu), (acc_hbm, acc))
        )
    ]
    for load in loads:
        load.start()

    barrier = pltpu.get_barrier_semaphore()
    for offset in (-2, -1, 1, 2):
        for tensor in range(2):
            pl.semaphore_signal(
                barrier, inc=1, device_id=(r, sec(offset), tensor), device_id_type=MESH
            )
    pl.semaphore_signal(barrier, inc=1, device_id=(r, s, other), device_id_type=MESH)
    for d in range(1, REPLICAS):
        pl.semaphore_signal(
            barrier, inc=1, device_id=(lax.rem(r + d, REPLICAS), s, t), device_id_type=MESH
        )
    pl.semaphore_wait(barrier, 9 + REPLICAS - 1)

    def cols(p):
        return pl.ds(p * WIDTH, WIDTH)

    up1 = [
        remote(down_hbm.at[:, cols(p)], wd1.at[:, cols(p)], up1_s.at[p], up1_r.at[p], sec(1), t)
        for p in range(PIECES)
    ]
    up2 = [
        remote(wd1.at[:, cols(p)], wd2.at[:, cols(p)], up2_s.at[p], up2_r.at[p], sec(1), t)
        for p in range(PIECES)
    ]
    dn = remote(up_hbm, wu1, dn_s, dn_r, sec(-1), t)
    for copy in up1:
        copy.start()
    dn.start()

    pre = pre_ref[...].astype(F32)
    sigma = jax.nn.sigmoid(pre)
    slope[...] = sigma * (1.0 + pre * (1.0 - sigma))
    hidden[...] = (pre * sigma).astype(BF)

    loads[0].wait()
    loads[1].wait()
    base_copy = remote(zbase, z.at[t], zb_s, zb_r, s, other)

    @pl.when(s >= SECTIONS - 3)
    def _():
        base = dot_t(cot[...], wd[...])
        zbase[...] = base
        base_copy.start()
        z[t] = base

    @pl.when(s == SECTIONS - 1)
    def _():
        g[...] = cot[...]
        q[...] = jnp.zeros_like(q)

    loads[2].wait()
    loads[3].wait()

    for p in range(PIECES):
        up1[p].wait_recv()
        up2[p].start()
    dn.wait_recv()
    m1s[...] = dot_t(wu[...], wd1[...])
    m2s[...] = dot_t(wu1[...], wd1[...])
    m1_copy = remote(m1s, m1.at[t], m1_s, m1_r, s, other)
    m2_copy = [remote(m2s, m2.at[t], m2_s.at[k], m2_r.at[t], sec(1), k) for k in range(2)]
    m2_from = [remote(m2s, m2.at[k], m2_s.at[k], m2_r.at[k], sec(1), k) for k in range(2)]
    m1_copy.start()
    for copy in m2_copy:
        copy.start()

    @pl.when(s >= SECTIONS - 3)
    def _():
        base_copy.wait()

    m1_copy.wait_recv()
    for copy in m2_from:
        copy.wait_recv()
    mcat[...] = jnp.concatenate([m1s[...] + m1[other], m2[0] + m2[1]], axis=1).astype(BF)

    def chunk_of(i):
        return pl.ds(pl.multiple_of(i * CHUNK, CHUNK), CHUNK)

    def q_copy(i):
        rows = chunk_of(i)
        return remote(qsend.at[rows], q.at[rows], q_s.at[i], q_r.at[i], sec(-1), t)

    def z_copy(i, k):
        rows = chunk_of(i)
        return remote(zsend.at[rows], z.at[t, rows], z_s.at[i, k], z_r.at[i, t], sec(-2), k)

    def z_from(i, k):
        rows = chunk_of(i)
        return remote(zsend.at[rows], z.at[k, rows], z_s.at[i, k], z_r.at[i, k], sec(-2), k)

    def g_copy(i, p):
        at = (chunk_of(i), cols(p))
        return remote(out.at[at], g.at[at], g_s.at[i, p], g_r.at[i, p], sec(-1), t)

    sends_q = s >= 2
    sends_z = jnp.logical_and(s >= 3, s <= SECTIONS - 2)

    def relay(i, _):
        rows = chunk_of(i)

        @pl.when(s >= 1)
        def _():
            @pl.when(s <= SECTIONS - 4)
            def _():
                z_from(i, 0).wait_recv()
                z_from(i, 1).wait_recv()

            @pl.when(s <= SECTIONS - 2)
            def _():
                q_copy(i).wait_recv()

            arrived = q[rows]
            total = z[0, rows] + z[1, rows] + arrived[:, :BAND]
            pre_grad = (total * slope[rows]).astype(BF)

            @pl.when(sends_q)
            def _():
                moved = jnp.concatenate(
                    [arrived[:, BAND:], jnp.zeros((CHUNK, BAND), F32)], axis=1
                )
                qsend[rows] = moved + dot(pre_grad, mcat[...])
                q_copy(i).start()

            for p in range(PIECES):
                @pl.when(s <= SECTIONS - 2)
                def _():
                    g_copy(i, p).wait_recv()

                passed = g[rows, cols(p)].astype(F32) + dot(pre_grad, wu[:, cols(p)])
                out[rows, cols(p)] = passed.astype(BF)
                g_copy(i, p).start()

        @pl.when(s == 0)
        def _():
            for p in range(PIECES):
                g_copy(i, p).wait_recv()

        @pl.when(sends_z)
        def _():
            @pl.when(i == 0)
            def _():
                for p in range(PIECES):
                    up2[p].wait_recv()

            zsend[rows] = dot_t(g[rows], wd2[...])
            for k in range(2):
                z_copy(i, k).start()

        return 0

    lax.fori_loop(0, CHUNKS, relay, 0)

    u_of = lax.broadcasted_iota(jnp.int32, (LOW, SPAN), 0)
    n_of = lax.broadcasted_iota(jnp.int32, (LOW, SPAN), 1)
    row_basis = basis(freqs_along(freq_ref, 0, u_of), n_of)
    u_t = lax.broadcasted_iota(jnp.int32, (SPAN, LOW), 1)
    n_t = lax.broadcasted_iota(jnp.int32, (SPAN, LOW), 0)
    row_basis_t = basis(freqs_along(freq_ref, 0, u_t), n_t)
    at_row = lax.broadcasted_iota(jnp.int32, (2 * SPAN, 2 * SPAN), 0)
    at_col = lax.broadcasted_iota(jnp.int32, (2 * SPAN, 2 * SPAN), 1)
    pair_basis = jnp.where(
        at_col // LOW == at_row // SPAN,
        basis(freqs_along(freq_ref, 1, lax.rem(at_col, LOW)), lax.rem(at_row, SPAN)),
        0.0,
    )

    grad = lax.dot_general(
        hidden[...], g[...], (((0,), (0,)), ((), ())), preferred_element_type=F32
    )
    moment = acc[...] + grad
    acc[...] = moment
    half = dot(row_basis, moment, HIGH)
    stacked = jnp.concatenate(
        [half[:, k * 2 * SPAN : (k + 1) * 2 * SPAN] for k in range(COLS // (2 * SPAN))], axis=0
    )
    coeffs = dot(stacked, pair_basis, HIGH)
    coef[...] = coeffs

    def share(k):
        return pl.ds(pl.multiple_of(k * 2 * LOW, 2 * LOW), 2 * LOW)

    def c_copy(d):
        to = lax.rem(r + d, REPLICAS)
        return pltpu.make_async_remote_copy(
            coef.at[share(to)], heard.at[d], c_s.at[d], c_r.at[d],
            device_id=(to, s, t), device_id_type=MESH,
        )

    for d in range(1, REPLICAS):
        c_copy(d).start()
    heard[0] = coef[share(r)]

    synced = flag_ref[0] == 1
    back = dot_t(coeffs, pair_basis, HIGH)
    wide = jnp.concatenate(
        [back[k * LOW : (k + 1) * LOW] for k in range(COLS // (2 * SPAN))], axis=1
    )
    decoded = dot(row_basis_t, wide, HIGH)
    moment = acc[...]
    res_ref[...] = jnp.where(synced, moment - decoded, moment)

    for p in range(PIECES):
        up1[p].wait_send()
        up2[p].wait_send()
    dn.wait_send()
    m1_copy.wait_send()
    for copy in m2_copy:
        copy.wait_send()

    @pl.when(jnp.logical_not(sends_z))
    def _():
        for p in range(PIECES):
            up2[p].wait_recv()

    def drain(i, _):
        @pl.when(sends_q)
        def _():
            q_copy(i).wait_send()

        @pl.when(sends_z)
        def _():
            for k in range(2):
                z_copy(i, k).wait_send()

        @pl.when(s >= 1)
        def _():
            for p in range(PIECES):
                g_copy(i, p).wait_send()

        return 0

    lax.fori_loop(0, CHUNKS, drain, 0)

    for d in range(1, REPLICAS):
        c_copy(d).wait_recv()
    summed = heard[0]
    for d in range(1, REPLICAS):
        summed = summed + heard[d]
    mean = summed * (1.0 / REPLICAS)
    back = dot_t(mean, pair_basis, HIGH)
    wide = jnp.concatenate([back[:LOW], back[LOW:]], axis=1)
    change = dot(row_basis_t, wide, HIGH)
    prior = outer_ref[...]
    moved = momentum_decay * prior + change
    stepped = -outer_rate * (change + momentum_decay * moved)
    new_ref[...] = jnp.where(synced, moved, prior)
    step_ref[...] = jnp.where(synced, stepped, jnp.zeros_like(stepped))
    for d in range(1, REPLICAS):
        c_copy(d).wait_send()


def local(
    cotangent, saved_pre, up_band, down_band, accumulated, outer_momentum, band_freqs, sync_flags
):
    vmem = pl.BlockSpec(memory_space=pltpu.VMEM)
    smem = pl.BlockSpec(memory_space=pltpu.SMEM)
    hbm = pl.BlockSpec(memory_space=pl.ANY)
    share = COLS // REPLICAS
    dma = pltpu.SemaphoreType.DMA
    residual, new_outer, outer_step = pl.pallas_call(
        kernel,
        out_shape=(
            jax.ShapeDtypeStruct((BAND, COLS), F32),
            jax.ShapeDtypeStruct((BAND, share), F32),
            jax.ShapeDtypeStruct((BAND, share), F32),
        ),
        in_specs=[smem, smem, hbm, vmem, hbm, hbm, hbm, vmem],
        out_specs=(vmem, vmem, vmem),
        scratch_shapes=[
            pltpu.VMEM((ROWS, COLS), BF),
            pltpu.VMEM((BAND, COLS), BF),
            pltpu.VMEM((BAND, COLS), BF),
            pltpu.VMEM((BAND, COLS), F32),
            pltpu.VMEM((ROWS, COLS), BF),
            pltpu.VMEM((ROWS, COLS), BF),
            pltpu.VMEM((BAND, COLS), BF),
            pltpu.VMEM((BAND, COLS), BF),
            pltpu.VMEM((BAND, COLS), BF),
            pltpu.VMEM((2, ROWS, BAND), F32),
            pltpu.VMEM((ROWS, BAND), F32),
            pltpu.VMEM((ROWS, BAND), F32),
            pltpu.VMEM((ROWS, 2 * BAND), F32),
            pltpu.VMEM((ROWS, 2 * BAND), F32),
            pltpu.VMEM((2, BAND, BAND), F32),
            pltpu.VMEM((2, BAND, BAND), F32),
            pltpu.VMEM((BAND, BAND), F32),
            pltpu.VMEM((BAND, BAND), F32),
            pltpu.VMEM((BAND, 2 * BAND), BF),
            pltpu.VMEM((ROWS, BAND), F32),
            pltpu.VMEM((ROWS, BAND), BF),
            pltpu.VMEM((REPLICAS * 2 * LOW, 2 * SPAN), F32),
            pltpu.VMEM((REPLICAS, 2 * LOW, 2 * SPAN), F32),
            dma((4,)),
            dma((PIECES,)), dma((PIECES,)), dma((PIECES,)), dma((PIECES,)),
            dma, dma, dma, dma,
            dma((2,)), dma((2,)),
            dma, dma,
            dma((CHUNKS, 2)), dma((CHUNKS, 2)),
            dma((CHUNKS,)), dma((CHUNKS,)),
            dma((CHUNKS, PIECES)), dma((CHUNKS, PIECES)),
            dma((REPLICAS,)), dma((REPLICAS,)),
        ],
        compiler_params=pltpu.CompilerParams(
            collective_id=0, has_side_effects=True, vmem_limit_bytes=48 << 20
        ),
        name="relay",
    )(
        band_freqs,
        sync_flags,
        cotangent.reshape(ROWS, COLS),
        saved_pre.reshape(ROWS, BAND),
        up_band[0],
        down_band[0],
        accumulated[0],
        outer_momentum[0, 0],
    )
    return (residual[None], new_outer[None, None], outer_step[None, None])


def solution(mesh):
    return jax.shard_map(
        local,
        mesh=mesh,
        in_specs=(
            P("replica", None, None, "tensor"),
            P("replica", "section", None, None, None),
            P("replica", "section", "tensor"),
            P("replica", "section", "tensor"),
            P("replica", "section", "tensor"),
            P("section", "tensor", None, "replica"),
            P(),
            P("section"),
        ),
        out_specs=(
            P("replica", "section", "tensor"),
            P("section", "tensor", None, "replica"),
            P("section", "tensor", None, "replica"),
        ),
        check_vma=False,
    )
```

```python
import math

import jax
import jax.numpy as jnp
from jax import lax
from jax.experimental import pallas as pl
from jax.experimental.pallas import tpu as pltpu
from jax.sharding import PartitionSpec as P

SPAN = 64
LOW = 8
momentum_decay = 0.9
outer_rate = 0.7

SECTIONS = 16
REPLICAS = 16
BAND = 64
COLS = 4096
ROWS = 192
CHUNK = 16
CHUNKS = ROWS // CHUNK
SHARE = COLS // (2 * SPAN) * LOW // REPLICAS
PIECES = 4
WIDTH = COLS // PIECES
PARTS = 4
PART = COLS // PARTS
HALF = CHUNK // 2
MESH = pl.DeviceIdType.MESH
HIGH = lax.Precision.HIGHEST
BF = jnp.bfloat16
F32 = jnp.float32


def dot(a, b, precision=None):
    return jnp.dot(a, b, preferred_element_type=F32, precision=precision)


def dot_t(a, b, precision=None):
    return lax.dot_general(
        a, b, (((1,), (1,)), ((), ())), preferred_element_type=F32, precision=precision
    )


def basis(freqs, position):
    turns = (freqs * (2 * position + 1)) & (4 * SPAN - 1)
    weight = jnp.where(freqs == 0, math.sqrt(1.0 / SPAN), math.sqrt(2.0 / SPAN))
    return weight * jnp.cos(turns.astype(F32) * (math.pi / (2 * SPAN)))


def freqs_along(freq_ref, row, which):
    out = jnp.zeros_like(which)
    for k in range(LOW):
        out = jnp.where(which == k, freq_ref[row, k], out)
    return out


def packed(block):
    return jnp.concatenate([block[:HALF], block[HALF:]], axis=1)


def unpacked(block):
    return jnp.concatenate([block[:, :BAND], block[:, BAND:]], axis=0)


def kernel(
    freq_ref, flag_ref, cot_hbm, pre_hbm, up_hbm, down_hbm, acc_hbm,
    delta_hbm, change_ref,
    cot, pre_ref, wu, wd, acc, g, out, wd1, wd2, wu1, z, za, zn, zf, q, qsend, m1, m2, m1s, m2s, near, far,
    slope, hidden, own, coef, heard,
    load_sem, up1_s, up1_r, up2_s, up2_r, dn_s, dn_r, m1_s, m1_r, m2_s, m2_r, zb_s, zb_r,
    za_s, zn_s, zf_s, z_r, q_s, q_r, g_s, g_r, c_s, c_r,
):
    r = lax.axis_index("replica")
    s = lax.axis_index("section")
    t = lax.axis_index("tensor")
    other = 1 - t
    top = SECTIONS - 1

    def sec(offset):
        return lax.rem(s + offset + SECTIONS, SECTIONS)

    def remote(src, dst, send, recv, section, tensor):
        return pltpu.make_async_remote_copy(
            src, dst, send, recv, device_id=(r, section, tensor), device_id_type=MESH
        )

    loads = [
        pltpu.make_async_copy(src, dst, load_sem.at[k])
        for k, (src, dst) in enumerate(
            (
                (pre_hbm, pre_ref),
                (down_hbm, wd),
                (cot_hbm, cot),
                (up_hbm, wu),
                (acc_hbm, acc),
            )
        )
    ]
    for load in loads:
        load.start()

    barrier = pltpu.get_barrier_semaphore()
    for offset in (-2, -1, 1, 2):
        for tensor in range(2):
            pl.semaphore_signal(
                barrier, inc=1, device_id=(r, sec(offset), tensor), device_id_type=MESH
            )
    pl.semaphore_signal(barrier, inc=1, device_id=(r, s, other), device_id_type=MESH)
    for d in range(1, REPLICAS):
        pl.semaphore_signal(
            barrier, inc=1, device_id=(lax.rem(r + d, REPLICAS), s, t), device_id_type=MESH
        )
    pl.semaphore_wait(barrier, 9 + REPLICAS - 1)

    def part(p):
        return pl.ds(p * PART, PART)

    up1 = [
        remote(down_hbm.at[:, part(p)], wd1.at[:, part(p)], up1_s.at[p], up1_r.at[p], sec(1), t)
        for p in range(PARTS)
    ]
    up2 = [
        remote(wd1.at[:, part(p)], wd2.at[:, part(p)], up2_s.at[p], up2_r.at[p], sec(1), t)
        for p in range(PARTS)
    ]
    dn = remote(up_hbm, wu1, dn_s, dn_r, sec(-1), t)
    for copy in up1:
        copy.start()
    dn.start()

    for load in loads[:4]:
        load.wait()
    base_copy = remote(za, z.at[t], zb_s, zb_r, s, other)

    @pl.when(s == top)
    def _():
        base = dot_t(cot[...], wd[...])
        for i in range(CHUNKS):
            za[pl.ds(i * HALF, HALF)] = packed(base[i * CHUNK : (i + 1) * CHUNK])
        base_copy.start()
        z[t] = za[...]

    pre = pre_ref[...].astype(F32)
    sigma = jax.nn.sigmoid(pre)
    slope[...] = sigma * (1.0 + pre * (1.0 - sigma))
    hidden[...] = (pre * sigma).astype(BF)

    def cols(p):
        return pl.ds(p * WIDTH, WIDTH)

    def chunk_of(i):
        return pl.ds(pl.multiple_of(i * CHUNK, CHUNK), CHUNK)

    def half_of(i):
        return pl.ds(pl.multiple_of(i * HALF, HALF), HALF)

    def q_copy(i):
        rows = half_of(i)
        return remote(qsend.at[rows], q.at[rows], q_s.at[i], q_r.at[i], sec(-1), t)

    def za_copy(i):
        rows = half_of(i)
        return remote(za.at[rows], z.at[t, rows], za_s.at[i], z_r.at[i, t], s, other)

    def zn_copy(i, k):
        rows = half_of(i)
        return remote(zn.at[rows], z.at[t, rows], zn_s.at[i, k], z_r.at[i, t], sec(-1), k)

    def zf_copy(i, k):
        rows = half_of(i)
        return remote(zf.at[rows], z.at[t, rows], zf_s.at[i, k], z_r.at[i, t], sec(-2), k)

    def z_from(i, k):
        rows = half_of(i)
        return remote(zf.at[rows], z.at[k, rows], zf_s.at[i, k], z_r.at[i, k], sec(-2), k)

    def g_copy(i, p):
        at = (chunk_of(i), cols(p))
        return remote(out.at[at], g.at[at], g_s.at[i, p], g_r.at[i, p], sec(-1), t)

    def add_own(i, p, entering, pre_grad):
        passed = entering.astype(F32) + own[:, cols(p)]
        out[chunk_of(i), cols(p)] = passed.astype(BF)
        g_copy(i, p).start()

    def pre_grad_of(i, from_above):
        total = z[0, half_of(i)] + z[1, half_of(i)]
        if from_above:
            total = total + q[half_of(i)]
        pre_grad = (unpacked(total) * slope[chunk_of(i)]).astype(BF)
        own[...] = dot(pre_grad, wu[...])
        return pre_grad

    def send_q(i, pre_grad):
        qsend[half_of(i)] = packed(dot(pre_grad, near[...]))
        q_copy(i).start()

    def send_near(i):
        zn[half_of(i)] = packed(dot_t(g[chunk_of(i)], wd1[...]))
        for k in range(2):
            zn_copy(i, k).start()

    @pl.when(s == top)
    def _():
        base_copy.wait()

        def first(i, _):
            pre_grad = pre_grad_of(i, False)
            for p in range(PIECES):
                add_own(i, p, cot[chunk_of(i), cols(p)], pre_grad)
            return 0

        lax.fori_loop(0, CHUNKS, first, 0)
        g[...] = cot[...]

    def own_base(i):
        for p in range(PIECES):
            g_copy(i, p).wait_recv()
        part_sum = packed(dot_t(g[chunk_of(i)], wd[...]))
        za[half_of(i)] = part_sum
        za_copy(i).start()
        z[t, half_of(i)] = part_sum

    def second(i):
        remote(za.at[half_of(i)], z.at[other, half_of(i)], za_s.at[i], z_r.at[i, other], s, other).wait_recv()
        pre_grad = pre_grad_of(i, False)
        for p in range(PIECES):
            add_own(i, p, g[chunk_of(i), cols(p)], pre_grad)
        return pre_grad

    @pl.when(s == top - 1)
    def _():
        own_base(0)
        own_base(1)

    for p in range(PARTS):
        up1[p].wait_recv()
        up2[p].start()
    m1s[...] = dot_t(wu[...], wd1[...])
    m1_copy = remote(m1s, m1.at[t], m1_s, m1_r, s, other)
    m1_copy.start()

    @pl.when(s == top - 1)
    def _():
        send_near(0)
        send_near(1)

    dn.wait_recv()
    m2s[...] = dot_t(wu1[...], wd1[...])
    m2_copy = [remote(m2s, m2.at[t], m2_s.at[k], m2_r.at[t], sec(1), k) for k in range(2)]
    m2_from = [remote(m2s, m2.at[k], m2_s.at[k], m2_r.at[k], sec(1), k) for k in range(2)]
    for copy in m2_copy:
        copy.start()

    @pl.when(s == top - 1)
    def _():
        qsend[half_of(0)] = packed(second(0).astype(F32))
        own_base(2)
        send_near(2)

    m1_copy.wait_recv()
    near[...] = (m1s[...] + m1[other]).astype(BF)

    @pl.when(s == top - 1)
    def _():
        send_q(0, unpacked(qsend[half_of(0)]).astype(BF))

        def rest(i, _):
            send_q(i, second(i))

            @pl.when(i < CHUNKS - 2)
            def _():
                own_base(i + 2)
                send_near(i + 2)

            return 0

        lax.fori_loop(1, CHUNKS, rest, 0)

    for copy in m2_from:
        copy.wait_recv()
    far[...] = (0.5 * (m2[0] + m2[1])).astype(BF)

    sends_q = jnp.logical_and(s >= 2, s <= top - 1)
    sends_near = jnp.logical_or(s == top - 1, s == top - 2)
    sends_far = jnp.logical_and(s >= 3, s <= top - 2)

    def relay(i, _):
        z_from(i, 0).wait_recv()
        z_from(i, 1).wait_recv()
        q_copy(i).wait_recv()
        pre_grad = pre_grad_of(i, True)

        @pl.when(s >= 2)
        def _():
            send_q(i, pre_grad)

        @pl.when(jnp.logical_and(s != top - 2, i == 0))
        def _():
            for p in range(PARTS):
                up2[p].wait_recv()

        for p in range(PIECES):
            g_copy(i, p).wait_recv()
            add_own(i, p, g[chunk_of(i), cols(p)], pre_grad)

        @pl.when(s == top - 2)
        def _():
            send_near(i)

            @pl.when(i == 0)
            def _():
                for p in range(PARTS):
                    up2[p].wait_recv()

        @pl.when(s >= 3)
        def _():
            ahead = dot(pre_grad, far[...]) + dot_t(g[chunk_of(i)], wd2[...])
            zf[half_of(i)] = packed(ahead)
            for k in range(2):
                zf_copy(i, k).start()

        return 0

    @pl.when(jnp.logical_and(s >= 1, s <= top - 2))
    def _():
        lax.fori_loop(0, CHUNKS, relay, 0)

    @pl.when(s == 0)
    def _():
        def last(i, _):
            for p in range(PIECES):
                g_copy(i, p).wait_recv()
            return 0

        lax.fori_loop(0, CHUNKS, last, 0)

    u_of = lax.broadcasted_iota(jnp.int32, (LOW, SPAN), 0)
    n_of = lax.broadcasted_iota(jnp.int32, (LOW, SPAN), 1)
    row_basis = basis(freqs_along(freq_ref, 0, u_of), n_of)
    u_t = lax.broadcasted_iota(jnp.int32, (SPAN, LOW), 1)
    n_t = lax.broadcasted_iota(jnp.int32, (SPAN, LOW), 0)
    row_basis_t = basis(freqs_along(freq_ref, 0, u_t), n_t)
    at_row = lax.broadcasted_iota(jnp.int32, (2 * SPAN, 2 * SPAN), 0)
    at_col = lax.broadcasted_iota(jnp.int32, (2 * SPAN, 2 * SPAN), 1)
    pair_basis = jnp.where(
        at_col // LOW == at_row // SPAN,
        basis(freqs_along(freq_ref, 1, lax.rem(at_col, LOW)), lax.rem(at_row, SPAN)),
        0.0,
    )

    loads[4].wait()
    grad = lax.dot_general(
        hidden[...], g[...], (((0,), (0,)), ((), ())), preferred_element_type=F32
    )
    moment = acc[...] + grad
    half = dot(row_basis, moment, HIGH)
    acc[...] = grad
    stacked = jnp.concatenate(
        [half[:, k * 2 * SPAN : (k + 1) * 2 * SPAN] for k in range(COLS // (2 * SPAN))], axis=0
    )
    coeffs = dot(stacked, pair_basis, HIGH)
    coef[...] = coeffs

    def share(k):
        return pl.ds(pl.multiple_of(k * SHARE, SHARE), SHARE)

    def c_copy(d):
        to = lax.rem(r + d, REPLICAS)
        return pltpu.make_async_remote_copy(
            coef.at[share(to)], heard.at[d], c_s.at[d], c_r.at[d],
            device_id=(to, s, t), device_id_type=MESH,
        )

    for d in range(1, REPLICAS):
        c_copy(d).start()
    heard[0] = coef[share(r)]

    synced = flag_ref[0] == 1
    back = dot_t(coeffs, pair_basis, HIGH)
    wide = jnp.concatenate(
        [back[k * LOW : (k + 1) * LOW] for k in range(COLS // (2 * SPAN))], axis=1
    )
    decoded = dot(row_basis_t, wide, HIGH)
    acc[...] = jnp.where(synced, acc[...] - decoded, acc[...])
    store = pltpu.make_async_copy(acc, delta_hbm, load_sem.at[5])
    store.start()

    for p in range(PARTS):
        up1[p].wait_send()
        up2[p].wait_send()
    dn.wait_send()
    m1_copy.wait_send()
    for copy in m2_copy:
        copy.wait_send()

    @pl.when(jnp.logical_not(sends_far))
    def _():
        @pl.when(jnp.logical_not(jnp.logical_and(s >= 1, s <= top - 2)))
        def _():
            for p in range(PARTS):
                up2[p].wait_recv()

    def drain(i, _):
        @pl.when(s == top - 1)
        def _():
            za_copy(i).wait_send()

        @pl.when(sends_near)
        def _():
            for k in range(2):
                zn_copy(i, k).wait_send()

        @pl.when(sends_far)
        def _():
            for k in range(2):
                zf_copy(i, k).wait_send()

        @pl.when(sends_q)
        def _():
            q_copy(i).wait_send()

        @pl.when(s >= 1)
        def _():
            for p in range(PIECES):
                g_copy(i, p).wait_send()

        return 0

    lax.fori_loop(0, CHUNKS, drain, 0)

    for d in range(1, REPLICAS):
        c_copy(d).wait_recv()
    summed = heard[0]
    for d in range(1, REPLICAS):
        summed = summed + heard[d]
    mean = summed * (1.0 / REPLICAS)
    back = dot_t(mean, pair_basis, HIGH)
    wide = jnp.concatenate([back[k * LOW : (k + 1) * LOW] for k in range(SHARE // LOW)], axis=1)
    change_ref[...] = dot(row_basis_t, wide, HIGH)
    store.wait()
    for d in range(1, REPLICAS):
        c_copy(d).wait_send()


def local(
    cotangent, saved_pre, up_band, down_band, accumulated, outer_momentum, band_freqs, sync_flags
):
    vmem = pl.BlockSpec(memory_space=pltpu.VMEM)
    smem = pl.BlockSpec(memory_space=pltpu.SMEM)
    hbm = pl.BlockSpec(memory_space=pl.ANY)
    share = COLS // REPLICAS
    dma = pltpu.SemaphoreType.DMA
    half_rows = ROWS // 2
    delta, change = pl.pallas_call(
        kernel,
        out_shape=(
            jax.ShapeDtypeStruct((BAND, COLS), F32),
            jax.ShapeDtypeStruct((BAND, share), F32),
        ),
        in_specs=[smem, smem, hbm, hbm, hbm, hbm, hbm],
        out_specs=(hbm, vmem),
        scratch_shapes=[
            pltpu.VMEM((ROWS, COLS), BF),
            pltpu.VMEM((ROWS, BAND), BF),
            pltpu.VMEM((BAND, COLS), BF),
            pltpu.VMEM((BAND, COLS), BF),
            pltpu.VMEM((BAND, COLS), F32),
            pltpu.VMEM((ROWS, COLS), BF),
            pltpu.VMEM((ROWS, COLS), BF),
            pltpu.VMEM((BAND, COLS), BF),
            pltpu.VMEM((BAND, COLS), BF),
            pltpu.VMEM((BAND, COLS), BF),
            pltpu.VMEM((2, half_rows, 2 * BAND), F32),
            pltpu.VMEM((half_rows, 2 * BAND), F32),
            pltpu.VMEM((half_rows, 2 * BAND), F32),
            pltpu.VMEM((half_rows, 2 * BAND), F32),
            pltpu.VMEM((half_rows, 2 * BAND), F32),
            pltpu.VMEM((half_rows, 2 * BAND), F32),
            pltpu.VMEM((2, BAND, BAND), F32),
            pltpu.VMEM((2, BAND, BAND), F32),
            pltpu.VMEM((BAND, BAND), F32),
            pltpu.VMEM((BAND, BAND), F32),
            pltpu.VMEM((BAND, BAND), BF),
            pltpu.VMEM((BAND, BAND), BF),
            pltpu.VMEM((ROWS, BAND), F32),
            pltpu.VMEM((ROWS, BAND), BF),
            pltpu.VMEM((CHUNK, COLS), F32),
            pltpu.VMEM((REPLICAS * SHARE, 2 * SPAN), F32),
            pltpu.VMEM((REPLICAS, SHARE, 2 * SPAN), F32),
            dma((6,)),
            dma((PARTS,)), dma((PARTS,)), dma((PARTS,)), dma((PARTS,)),
            dma, dma, dma, dma,
            dma((2,)), dma((2,)),
            dma, dma,
            dma((CHUNKS,)), dma((CHUNKS, 2)), dma((CHUNKS, 2)), dma((CHUNKS, 2)),
            dma((CHUNKS,)), dma((CHUNKS,)),
            dma((CHUNKS, PIECES)), dma((CHUNKS, PIECES)),
            dma((REPLICAS,)), dma((REPLICAS,)),
        ],
        compiler_params=pltpu.CompilerParams(
            collective_id=0, has_side_effects=True, vmem_limit_bytes=60 << 20
        ),
        name="relay",
    )(
        band_freqs,
        sync_flags,
        cotangent.reshape(ROWS, COLS),
        saved_pre.reshape(ROWS, BAND),
        up_band[0],
        down_band[0],
        accumulated[0],
    )
    residual = accumulated + delta[None]
    synced = sync_flags[0] == 1
    prior = outer_momentum[0, 0]
    moved = momentum_decay * prior + change
    stepped = -outer_rate * (change + momentum_decay * moved)
    new_outer = jnp.where(synced, moved, prior)
    outer_step = jnp.where(synced, stepped, jnp.zeros_like(stepped))
    return (residual, new_outer[None, None], outer_step[None, None])


def solution(mesh):
    return jax.shard_map(
        local,
        mesh=mesh,
        in_specs=(
            P("replica", None, None, "tensor"),
            P("replica", "section", None, None, None),
            P("replica", "section", "tensor"),
            P("replica", "section", "tensor"),
            P("replica", "section", "tensor"),
            P("section", "tensor", None, "replica"),
            P(),
            P("section"),
        ),
        out_specs=(
            P("replica", "section", "tensor"),
            P("section", "tensor", None, "replica"),
            P("section", "tensor", None, "replica"),
        ),
        check_vma=False,
    )
```

```python
import math

import jax
import jax.numpy as jnp
from jax import lax
from jax.experimental import pallas as pl
from jax.experimental.pallas import tpu as pltpu
from jax.sharding import PartitionSpec as P

SPAN = 64
LOW = 8
momentum_decay = 0.9
outer_rate = 0.7

SECTIONS = 16
REPLICAS = 16
BAND = 64
COLS = 4096
ROWS = 192
CHUNK = 16
CHUNKS = ROWS // CHUNK
SHARE = COLS // (2 * SPAN) * LOW // REPLICAS
PIECES = 4
LIMIT = 60
GROUPS = 3
GROUP = ROWS // GROUPS
WIDTH = COLS // PIECES
PARTS = 4
PART = COLS // PARTS
HALF = CHUNK // 2
MESH = pl.DeviceIdType.MESH
HIGH = lax.Precision.HIGHEST
BF = jnp.bfloat16
F32 = jnp.float32


def dot(a, b, precision=None):
    return jnp.dot(a, b, preferred_element_type=F32, precision=precision)


def dot_t(a, b, precision=None):
    return lax.dot_general(
        a, b, (((1,), (1,)), ((), ())), preferred_element_type=F32, precision=precision
    )


def basis(freqs, position):
    turns = (freqs * (2 * position + 1)) & (4 * SPAN - 1)
    weight = jnp.where(freqs == 0, math.sqrt(1.0 / SPAN), math.sqrt(2.0 / SPAN))
    return weight * jnp.cos(turns.astype(F32) * (math.pi / (2 * SPAN)))


def freqs_along(freq_ref, row, which):
    out = jnp.zeros_like(which)
    for k in range(LOW):
        out = jnp.where(which == k, freq_ref[row, k], out)
    return out


def packed(block):
    return jnp.concatenate([block[:HALF], block[HALF:]], axis=1).astype(BF)


def unpacked(block):
    return jnp.concatenate([block[:, :BAND], block[:, BAND:]], axis=0)


def kernel(
    freq_hbm, flag_hbm, cot_hbm, pre_hbm, up_hbm, down_hbm, acc_hbm,
    delta_ref, change_ref,
    freq_ref, flag_ref, row_ref, row_t_ref, pair_ref,
    cot, pre_ref, wu, wd, acc, g, out, wd1, wd2, wu1, z, za, zn, zf, q, qsend, m1, m2, m1s, m2s, near, far,
    slope, hidden, own, kept, coef, heard,
    load_sem, up1_s, up1_r, up2_s, up2_r, dn_s, dn_r, m1_s, m1_r, m2_s, m2_r, zb_s, zb_r,
    za_s, zn_s, zf_s, z_r, q_s, q_r, g_s, g_r, c_s, c_r,
):
    r = lax.axis_index("replica")
    s = lax.axis_index("section")
    t = lax.axis_index("tensor")
    other = 1 - t
    top = SECTIONS - 1

    def sec(offset):
        return lax.rem(s + offset + SECTIONS, SECTIONS)

    def remote(src, dst, send, recv, section, tensor):
        return pltpu.make_async_remote_copy(
            src, dst, send, recv, device_id=(r, section, tensor), device_id_type=MESH
        )

    loads = [
        pltpu.make_async_copy(src, dst, load_sem.at[k])
        for k, (src, dst) in enumerate(
            (
                (pre_hbm, pre_ref),
                (down_hbm, wd),
                (cot_hbm, cot),
                (up_hbm, wu),
                (acc_hbm, acc),
                (freq_hbm, freq_ref),
                (flag_hbm, flag_ref),
            )
        )
    ]
    for load in loads:
        load.start()

    barrier = pltpu.get_barrier_semaphore()
    for offset in (-2, -1, 1, 2):
        for tensor in range(2):
            pl.semaphore_signal(
                barrier, inc=1, device_id=(r, sec(offset), tensor), device_id_type=MESH
            )
    pl.semaphore_signal(barrier, inc=1, device_id=(r, s, other), device_id_type=MESH)
    for d in range(1, REPLICAS):
        pl.semaphore_signal(
            barrier, inc=1, device_id=(lax.rem(r + d, REPLICAS), s, t), device_id_type=MESH
        )
    pl.semaphore_wait(barrier, 9 + REPLICAS - 1)

    def part(p):
        return pl.ds(p * PART, PART)

    up1 = [
        remote(down_hbm.at[:, part(p)], wd1.at[:, part(p)], up1_s.at[p], up1_r.at[p], sec(1), t)
        for p in range(PARTS)
    ]
    up2 = [
        remote(wd1.at[:, part(p)], wd2.at[:, part(p)], up2_s.at[p], up2_r.at[p], sec(1), t)
        for p in range(PARTS)
    ]
    dn = remote(up_hbm, wu1, dn_s, dn_r, sec(-1), t)
    for copy in up1:
        copy.start()

    sends_dn = s <= top - 2
    takes_dn = jnp.logical_or(s <= top - 3, s == top)

    @pl.when(sends_dn)
    def _():
        dn.start()

    for load in loads[:4]:
        load.wait()

    def base_rows(k):
        return pl.ds(k * (GROUP // CHUNK), GROUP // CHUNK)

    base_copy = [
        remote(za.at[base_rows(k)], z.at[t, base_rows(k)], zb_s.at[k], zb_r.at[k], s, other)
        for k in range(GROUPS)
    ]
    base_from = [
        remote(za.at[base_rows(k)], z.at[other, base_rows(k)], zb_s.at[k], zb_r.at[k], s, other)
        for k in range(GROUPS)
    ]

    @pl.when(s == top)
    def _():
        for k in range(GROUPS):
            base = dot_t(cot[pl.ds(k * GROUP, GROUP)], wd[...])
            for i in range(GROUP // CHUNK):
                za[k * (GROUP // CHUNK) + i] = packed(base[i * CHUNK : (i + 1) * CHUNK])
            base_copy[k].start()
            z[t, base_rows(k)] = za[base_rows(k)]

    pre = pre_ref[...].astype(F32)
    sigma = jax.nn.sigmoid(pre)
    slope[...] = sigma * (1.0 + pre * (1.0 - sigma))
    hidden[...] = (pre * sigma).astype(BF)

    for load in loads[5:]:
        load.wait()
    u_of = lax.broadcasted_iota(jnp.int32, (LOW, SPAN), 0)
    n_of = lax.broadcasted_iota(jnp.int32, (LOW, SPAN), 1)
    row_ref[...] = basis(freqs_along(freq_ref, 0, u_of), n_of)
    u_t = lax.broadcasted_iota(jnp.int32, (SPAN, LOW), 1)
    n_t = lax.broadcasted_iota(jnp.int32, (SPAN, LOW), 0)
    row_t_ref[...] = basis(freqs_along(freq_ref, 0, u_t), n_t)
    at_row = lax.broadcasted_iota(jnp.int32, (2 * SPAN, 2 * SPAN), 0)
    at_col = lax.broadcasted_iota(jnp.int32, (2 * SPAN, 2 * SPAN), 1)
    pair_ref[...] = jnp.where(
        at_col // LOW == at_row // SPAN,
        basis(freqs_along(freq_ref, 1, lax.rem(at_col, LOW)), lax.rem(at_row, SPAN)),
        0.0,
    )

    def cols(p):
        return pl.ds(p * WIDTH, WIDTH)

    def chunk_of(i):
        return pl.ds(pl.multiple_of(i * CHUNK, CHUNK), CHUNK)

    def q_copy(i):
        return remote(qsend.at[i], q.at[i], q_s.at[i], q_r.at[i], sec(-1), t)

    def za_copy(i):
        return remote(za.at[i], z.at[t, i], za_s.at[i], z_r.at[i, t], s, other)

    def zn_copy(i, k):
        return remote(zn.at[i], z.at[t, i], zn_s.at[i, k], z_r.at[i, t], sec(-1), k)

    def zf_copy(i, k):
        return remote(zf.at[i], z.at[t, i], zf_s.at[i, k], z_r.at[i, t], sec(-2), k)

    def z_from(i, k):
        return remote(zf.at[i], z.at[k, i], zf_s.at[i, k], z_r.at[i, k], sec(-2), k)

    def g_copy(i, p):
        at = (chunk_of(i), cols(p))
        return remote(out.at[at], g.at[at], g_s.at[i, p], g_r.at[i, p], sec(-1), t)

    def add_own(i, p, entering):
        passed = entering.astype(F32) + own[:, cols(p)]
        out[chunk_of(i), cols(p)] = passed.astype(BF)
        g_copy(i, p).start()

    def pre_grad_of(i, from_above):
        total = z[0, i].astype(F32) + z[1, i].astype(F32)
        if from_above:
            total = total + q[i].astype(F32)
        return (unpacked(total) * slope[chunk_of(i)]).astype(BF)

    def own_term(pre_grad):
        own[...] = dot(pre_grad, wu[...])

    def send_q(i, pre_grad):
        qsend[i] = packed(dot(pre_grad, near[...]))
        q_copy(i).start()

    def send_near(i):
        zn[i] = packed(dot_t(g[chunk_of(i)], wd1[...]))
        for k in range(2):
            zn_copy(i, k).start()

    @pl.when(s == top)
    def _():
        def first(i, _):
            own_term(pre_grad_of(i, False))
            for p in range(PIECES):
                add_own(i, p, cot[chunk_of(i), cols(p)])
            return 0

        for k in range(GROUPS):
            base_from[k].wait_recv()
            lax.fori_loop(k * GROUP // CHUNK, (k + 1) * GROUP // CHUNK, first, 0)
        for k in range(GROUPS):
            base_copy[k].wait_send()
        g[...] = cot[...]

    def own_base(i):
        for p in range(PIECES):
            g_copy(i, p).wait_recv()
        part_sum = packed(dot_t(g[chunk_of(i)], wd[...]))
        za[i] = part_sum
        za_copy(i).start()
        z[t, i] = part_sum

    def second(i):
        remote(za.at[i], z.at[other, i], za_s.at[i], z_r.at[i, other], s, other).wait_recv()
        pre_grad = pre_grad_of(i, False)
        own_term(pre_grad)
        for p in range(PIECES):
            add_own(i, p, g[chunk_of(i), cols(p)])
        return pre_grad

    @pl.when(s == top - 1)
    def _():
        own_base(0)
        own_base(1)

    for p in range(PARTS):
        up1[p].wait_recv()
        up2[p].start()
    m1s[...] = dot_t(wu[...], wd1[...])
    m1_copy = remote(m1s, m1.at[t], m1_s, m1_r, s, other)
    m1_copy.start()

    @pl.when(s == top - 1)
    def _():
        send_near(0)
        send_near(1)

    @pl.when(takes_dn)
    def _():
        dn.wait_recv()
        m2s[...] = dot_t(wu1[...], wd1[...])

    @pl.when(jnp.logical_not(takes_dn))
    def _():
        m2s[...] = jnp.zeros_like(m2s)

    m2_copy = [remote(m2s, m2.at[t], m2_s.at[k], m2_r.at[t], sec(1), k) for k in range(2)]
    m2_from = [remote(m2s, m2.at[k], m2_s.at[k], m2_r.at[k], sec(1), k) for k in range(2)]
    for copy in m2_copy:
        copy.start()

    @pl.when(s == top - 1)
    def _():
        kept[...] = second(0)
        own_base(2)
        send_near(2)

    m1_copy.wait_recv()
    near[...] = (m1s[...] + m1[other]).astype(BF)

    @pl.when(s == top - 1)
    def _():
        send_q(0, kept[...])

        def rest(i, _):
            send_q(i, second(i))

            @pl.when(i < CHUNKS - 2)
            def _():
                own_base(i + 2)
                send_near(i + 2)

            return 0

        lax.fori_loop(1, CHUNKS, rest, 0)

    for copy in m2_from:
        copy.wait_recv()
    far[...] = (0.5 * (m2[0] + m2[1])).astype(BF)

    sends_q = jnp.logical_and(s >= 2, s <= top - 1)
    sends_near = jnp.logical_or(s == top - 1, s == top - 2)
    sends_far = jnp.logical_and(s >= 3, s <= top - 2)

    def send_far(i, ahead):
        zf[i] = packed(ahead)
        for k in range(2):
            zf_copy(i, k).start()

    def arrive(i):
        z_from(i, 0).wait_recv()
        z_from(i, 1).wait_recv()
        q_copy(i).wait_recv()
        return pre_grad_of(i, True)

    @pl.when(s == top - 2)
    def _():
        def third(i, _):
            pre_grad = arrive(i)
            send_q(i, pre_grad)
            own_term(pre_grad)
            for p in range(PIECES):
                g_copy(i, p).wait_recv()
                add_own(i, p, g[chunk_of(i), cols(p)])
            send_near(i)

            @pl.when(i == 0)
            def _():
                for p in range(PARTS):
                    up2[p].wait_recv()

            send_far(i, dot(pre_grad, far[...]) + dot_t(g[chunk_of(i)], wd2[...]))
            return 0

        lax.fori_loop(0, CHUNKS, third, 0)

    @pl.when(jnp.logical_and(s >= 1, s <= top - 3))
    def _():
        for p in range(PARTS):
            up2[p].wait_recv()

        def relay(i, _):
            pre_grad = arrive(i)

            @pl.when(s >= 2)
            def _():
                send_q(i, pre_grad)

            own_term(pre_grad)
            ahead = dot(pre_grad, far[...])
            for p in range(PIECES):
                g_copy(i, p).wait_recv()
                entering = g[chunk_of(i), cols(p)]
                if p < PIECES - 1:
                    add_own(i, p, entering)
                ahead = ahead + dot_t(entering, wd2[:, cols(p)])

            @pl.when(s >= 3)
            def _():
                send_far(i, ahead)

            add_own(i, PIECES - 1, entering)
            return 0

        lax.fori_loop(0, CHUNKS, relay, 0)

    @pl.when(s == 0)
    def _():
        def last(i, _):
            for p in range(PIECES):
                g_copy(i, p).wait_recv()
            return 0

        lax.fori_loop(0, CHUNKS, last, 0)

    loads[4].wait()
    row_basis, row_basis_t, pair_basis = row_ref[...], row_t_ref[...], pair_ref[...]
    grad = lax.dot_general(
        hidden[...], g[...], (((0,), (0,)), ((), ())), preferred_element_type=F32
    )
    moment = acc[...] + grad
    half = dot(row_basis, moment, HIGH)
    acc[...] = grad
    stacked = jnp.concatenate(
        [half[:, k * 2 * SPAN : (k + 1) * 2 * SPAN] for k in range(COLS // (2 * SPAN))], axis=0
    )
    coeffs = dot(stacked, pair_basis, HIGH)
    coef[...] = coeffs

    def share(k):
        return pl.ds(pl.multiple_of(k * SHARE, SHARE), SHARE)

    def c_copy(d):
        to = lax.rem(r + d, REPLICAS)
        return pltpu.make_async_remote_copy(
            coef.at[share(to)], heard.at[d], c_s.at[d], c_r.at[d],
            device_id=(to, s, t), device_id_type=MESH,
        )

    for d in range(1, REPLICAS):
        c_copy(d).start()
    heard[0] = coef[share(r)]

    synced = flag_ref[0] == 1
    back = dot_t(coeffs, pair_basis, HIGH)
    wide = jnp.concatenate(
        [back[k * LOW : (k + 1) * LOW] for k in range(COLS // (2 * SPAN))], axis=1
    )
    decoded = dot(row_basis_t, wide, HIGH)
    delta_ref[...] = jnp.where(synced, acc[...] - decoded, acc[...])

    for p in range(PARTS):
        up1[p].wait_send()
        up2[p].wait_send()

    @pl.when(sends_dn)
    def _():
        dn.wait_send()

    m1_copy.wait_send()
    for copy in m2_copy:
        copy.wait_send()

    @pl.when(jnp.logical_not(sends_far))
    def _():
        @pl.when(jnp.logical_not(jnp.logical_and(s >= 1, s <= top - 2)))
        def _():
            for p in range(PARTS):
                up2[p].wait_recv()

    def drain(i, _):
        @pl.when(s == top - 1)
        def _():
            za_copy(i).wait_send()

        @pl.when(sends_near)
        def _():
            for k in range(2):
                zn_copy(i, k).wait_send()

        @pl.when(sends_far)
        def _():
            for k in range(2):
                zf_copy(i, k).wait_send()

        @pl.when(sends_q)
        def _():
            q_copy(i).wait_send()

        @pl.when(s >= 1)
        def _():
            for p in range(PIECES):
                g_copy(i, p).wait_send()

        return 0

    lax.fori_loop(0, CHUNKS, drain, 0)

    for d in range(1, REPLICAS):
        c_copy(d).wait_recv()
    summed = heard[0]
    for d in range(1, REPLICAS):
        summed = summed + heard[d]
    mean = summed * (1.0 / REPLICAS)
    back = dot_t(mean, pair_basis, HIGH)
    wide = jnp.concatenate([back[k * LOW : (k + 1) * LOW] for k in range(SHARE // LOW)], axis=1)
    change_ref[...] = dot(row_basis_t, wide, HIGH)
    for d in range(1, REPLICAS):
        c_copy(d).wait_send()


def local(
    cotangent, saved_pre, up_band, down_band, accumulated, outer_momentum, band_freqs, sync_flags
):
    vmem = pl.BlockSpec(memory_space=pltpu.VMEM)
    hbm = pl.BlockSpec(memory_space=pltpu.HBM)
    share = COLS // REPLICAS
    dma = pltpu.SemaphoreType.DMA
    delta, change = pl.pallas_call(
        kernel,
        out_shape=(
            jax.ShapeDtypeStruct((BAND, COLS), F32),
            jax.ShapeDtypeStruct((BAND, share), F32),
        ),
        in_specs=[hbm] * 7,
        out_specs=(vmem, vmem),
        scratch_shapes=[
            pltpu.SMEM((2, LOW), jnp.int32),
            pltpu.SMEM((1,), jnp.int32),
            pltpu.VMEM((LOW, SPAN), F32),
            pltpu.VMEM((SPAN, LOW), F32),
            pltpu.VMEM((2 * SPAN, 2 * SPAN), F32),
            pltpu.VMEM((ROWS, COLS), BF),
            pltpu.VMEM((ROWS, BAND), BF),
            pltpu.VMEM((BAND, COLS), BF),
            pltpu.VMEM((BAND, COLS), BF),
            pltpu.VMEM((BAND, COLS), F32),
            pltpu.VMEM((ROWS, COLS), BF),
            pltpu.VMEM((ROWS, COLS), BF),
            pltpu.VMEM((BAND, COLS), BF),
            pltpu.VMEM((BAND, COLS), BF),
            pltpu.VMEM((BAND, COLS), BF),
            pltpu.VMEM((2, CHUNKS, HALF, 2 * BAND), BF),
            pltpu.VMEM((CHUNKS, HALF, 2 * BAND), BF),
            pltpu.VMEM((CHUNKS, HALF, 2 * BAND), BF),
            pltpu.VMEM((CHUNKS, HALF, 2 * BAND), BF),
            pltpu.VMEM((CHUNKS, HALF, 2 * BAND), BF),
            pltpu.VMEM((CHUNKS, HALF, 2 * BAND), BF),
            pltpu.VMEM((2, BAND, BAND), F32),
            pltpu.VMEM((2, BAND, BAND), F32),
            pltpu.VMEM((BAND, BAND), F32),
            pltpu.VMEM((BAND, BAND), F32),
            pltpu.VMEM((BAND, BAND), BF),
            pltpu.VMEM((BAND, BAND), BF),
            pltpu.VMEM((ROWS, BAND), F32),
            pltpu.VMEM((ROWS, BAND), BF),
            pltpu.VMEM((CHUNK, COLS), F32),
            pltpu.VMEM((CHUNK, BAND), BF),
            pltpu.VMEM((REPLICAS * SHARE, 2 * SPAN), F32),
            pltpu.VMEM((REPLICAS, SHARE, 2 * SPAN), F32),
            dma((7,)),
            dma((PARTS,)), dma((PARTS,)), dma((PARTS,)), dma((PARTS,)),
            dma, dma, dma, dma,
            dma((2,)), dma((2,)),
            dma((GROUPS,)), dma((GROUPS,)),
            dma((CHUNKS,)), dma((CHUNKS, 2)), dma((CHUNKS, 2)), dma((CHUNKS, 2)),
            dma((CHUNKS,)), dma((CHUNKS,)),
            dma((CHUNKS, PIECES)), dma((CHUNKS, PIECES)),
            dma((REPLICAS,)), dma((REPLICAS,)),
        ],
        compiler_params=pltpu.CompilerParams(
            collective_id=0, has_side_effects=True, vmem_limit_bytes=LIMIT << 20
        ),
        name="relay",
    )(
        band_freqs,
        sync_flags,
        cotangent.reshape(ROWS, COLS),
        saved_pre.reshape(ROWS, BAND),
        up_band[0],
        down_band[0],
        accumulated[0],
    )
    residual = accumulated + delta[None]
    synced = sync_flags[0] == 1
    prior = outer_momentum[0, 0]
    moved = momentum_decay * prior + change
    stepped = -outer_rate * (change + momentum_decay * moved)
    new_outer = jnp.where(synced, moved, prior)
    outer_step = jnp.where(synced, stepped, jnp.zeros_like(stepped))
    return (residual, new_outer[None, None], outer_step[None, None])


def solution(mesh):
    return jax.shard_map(
        local,
        mesh=mesh,
        in_specs=(
            P("replica", None, None, "tensor"),
            P("replica", "section", None, None, None),
            P("replica", "section", "tensor"),
            P("replica", "section", "tensor"),
            P("replica", "section", "tensor"),
            P("section", "tensor", None, "replica"),
            P(),
            P("section"),
        ),
        out_specs=(
            P("replica", "section", "tensor"),
            P("section", "tensor", None, "replica"),
            P("section", "tensor", None, "replica"),
        ),
        check_vma=False,
    )
```

```python
import math

import jax
import jax.numpy as jnp
from jax import lax
from jax.experimental import pallas as pl
from jax.experimental.pallas import tpu as pltpu
from jax.sharding import PartitionSpec as P

SPAN = 64
LOW = 8
momentum_decay = 0.9
outer_rate = 0.7

SECTIONS = 16
REPLICAS = 16
BAND = 64
COLS = 4096
ROWS = 192
CHUNK = 16
CHUNKS = ROWS // CHUNK
SHARE = COLS // (2 * SPAN) * LOW // REPLICAS
PIECES = 4
LIMIT = 60
GROUPS = 3
GROUP = ROWS // GROUPS
WIDTH = COLS // PIECES
PARTS = 4
PART = COLS // PARTS
HALF = CHUNK // 2
MESH = pl.DeviceIdType.MESH
HIGH = lax.Precision.HIGHEST
BF = jnp.bfloat16
F32 = jnp.float32


def dot(a, b, precision=None):
    return jnp.dot(a, b, preferred_element_type=F32, precision=precision)


def dot_t(a, b, precision=None):
    return lax.dot_general(
        a, b, (((1,), (1,)), ((), ())), preferred_element_type=F32, precision=precision
    )


def basis(freqs, position):
    turns = (freqs * (2 * position + 1)) & (4 * SPAN - 1)
    weight = jnp.where(freqs == 0, math.sqrt(1.0 / SPAN), math.sqrt(2.0 / SPAN))
    return weight * jnp.cos(turns.astype(F32) * (math.pi / (2 * SPAN)))


def freqs_along(freq_ref, row, which):
    out = jnp.zeros_like(which)
    for k in range(LOW):
        out = jnp.where(which == k, freq_ref[row, k], out)
    return out


def packed(block):
    return jnp.concatenate([block[:HALF], block[HALF:]], axis=1).astype(BF)


def unpacked(block):
    return jnp.concatenate([block[:, :BAND], block[:, BAND:]], axis=0)


def kernel(
    freq_hbm, flag_hbm, cot_hbm, pre_hbm, up_hbm, down_hbm, acc_hbm,
    delta_ref, change_ref,
    freq_ref, flag_ref, row_ref, row_t_ref, pair_ref,
    cot, pre_ref, wu, wd, acc, g, out, wd1, wd2, wu1, z, za, zn, zf, q, qsend, m1, m2, m1s, m2s, near, far,
    slope, hidden, own, kept, coef, heard,
    load_sem, up1_s, up1_r, up2_s, up2_r, dn_s, dn_r, m1_s, m1_r, m2_s, m2_r, zb_s, zb_r,
    za_s, zn_s, zf_s, z_r, q_s, q_r, g_s, g_r, c_s, c_r,
):
    r = lax.axis_index("replica")
    s = lax.axis_index("section")
    t = lax.axis_index("tensor")
    other = 1 - t
    top = SECTIONS - 1

    def sec(offset):
        return lax.rem(s + offset + SECTIONS, SECTIONS)

    def remote(src, dst, send, recv, section, tensor):
        return pltpu.make_async_remote_copy(
            src, dst, send, recv, device_id=(r, section, tensor), device_id_type=MESH
        )

    loads = [
        pltpu.make_async_copy(src, dst, load_sem.at[k])
        for k, (src, dst) in enumerate(
            (
                (pre_hbm, pre_ref),
                (down_hbm, wd),
                (cot_hbm, cot),
                (up_hbm, wu),
                (acc_hbm, acc),
                (freq_hbm, freq_ref),
                (flag_hbm, flag_ref),
            )
        )
    ]
    for load in loads:
        load.start()

    barrier = pltpu.get_barrier_semaphore()
    for offset in (-2, -1, 1, 2):
        for tensor in range(2):
            pl.semaphore_signal(
                barrier, inc=1, device_id=(r, sec(offset), tensor), device_id_type=MESH
            )
    pl.semaphore_signal(barrier, inc=1, device_id=(r, s, other), device_id_type=MESH)
    for d in range(1, REPLICAS):
        pl.semaphore_signal(
            barrier, inc=1, device_id=(lax.rem(r + d, REPLICAS), s, t), device_id_type=MESH
        )
    pl.semaphore_wait(barrier, 9 + REPLICAS - 1)

    def part(p):
        return pl.ds(p * PART, PART)

    up1 = [
        remote(down_hbm.at[:, part(p)], wd1.at[:, part(p)], up1_s.at[p], up1_r.at[p], sec(1), t)
        for p in range(PARTS)
    ]
    up2 = [
        remote(wd1.at[:, part(p)], wd2.at[:, part(p)], up2_s.at[p], up2_r.at[p], sec(1), t)
        for p in range(PARTS)
    ]
    dn = remote(up_hbm, wu1, dn_s, dn_r, sec(-1), t)
    for copy in up1:
        copy.start()

    sends_dn = s <= top - 2
    takes_dn = jnp.logical_or(s <= top - 3, s == top)

    @pl.when(sends_dn)
    def _():
        dn.start()

    for load in loads[:4]:
        load.wait()

    def base_rows(k):
        return pl.ds(k * (GROUP // CHUNK), GROUP // CHUNK)

    base_copy = [
        remote(za.at[base_rows(k)], z.at[t, base_rows(k)], zb_s.at[k], zb_r.at[k], s, other)
        for k in range(GROUPS)
    ]
    base_from = [
        remote(za.at[base_rows(k)], z.at[other, base_rows(k)], zb_s.at[k], zb_r.at[k], s, other)
        for k in range(GROUPS)
    ]

    @pl.when(s == top)
    def _():
        for k in range(GROUPS):
            base = dot_t(cot[pl.ds(k * GROUP, GROUP)], wd[...])
            for i in range(GROUP // CHUNK):
                za[k * (GROUP // CHUNK) + i] = packed(base[i * CHUNK : (i + 1) * CHUNK])
            base_copy[k].start()
            z[t, base_rows(k)] = za[base_rows(k)]

    pre = pre_ref[...].astype(F32)
    sigma = jax.nn.sigmoid(pre)
    slope[...] = sigma * (1.0 + pre * (1.0 - sigma))
    hidden[...] = (pre * sigma).astype(BF)

    for load in loads[5:]:
        load.wait()
    u_of = lax.broadcasted_iota(jnp.int32, (LOW, SPAN), 0)
    n_of = lax.broadcasted_iota(jnp.int32, (LOW, SPAN), 1)
    row_ref[...] = basis(freqs_along(freq_ref, 0, u_of), n_of)
    u_t = lax.broadcasted_iota(jnp.int32, (SPAN, LOW), 1)
    n_t = lax.broadcasted_iota(jnp.int32, (SPAN, LOW), 0)
    row_t_ref[...] = basis(freqs_along(freq_ref, 0, u_t), n_t)
    at_row = lax.broadcasted_iota(jnp.int32, (2 * SPAN, 2 * SPAN), 0)
    at_col = lax.broadcasted_iota(jnp.int32, (2 * SPAN, 2 * SPAN), 1)
    pair_ref[...] = jnp.where(
        at_col // LOW == at_row // SPAN,
        basis(freqs_along(freq_ref, 1, lax.rem(at_col, LOW)), lax.rem(at_row, SPAN)),
        0.0,
    )

    def cols(p):
        return pl.ds(p * WIDTH, WIDTH)

    def chunk_of(i):
        return pl.ds(pl.multiple_of(i * CHUNK, CHUNK), CHUNK)

    def q_copy(i):
        return remote(qsend.at[i], q.at[i], q_s.at[i], q_r.at[i], sec(-1), t)

    def za_copy(i):
        return remote(za.at[i], z.at[t, i], za_s.at[i], z_r.at[i, t], s, other)

    def zn_copy(i, k):
        return remote(zn.at[i], z.at[t, i], zn_s.at[i, k], z_r.at[i, t], sec(-1), k)

    def zf_copy(i, k):
        return remote(zf.at[i], z.at[t, i], zf_s.at[i, k], z_r.at[i, t], sec(-2), k)

    def z_from(i, k):
        return remote(zf.at[i], z.at[k, i], zf_s.at[i, k], z_r.at[i, k], sec(-2), k)

    def g_copy(i, p):
        at = (chunk_of(i), cols(p))
        return remote(out.at[at], g.at[at], g_s.at[i, p], g_r.at[i, p], sec(-1), t)

    def add_own(i, p, entering):
        passed = entering.astype(F32) + own[:, cols(p)]
        out[chunk_of(i), cols(p)] = passed.astype(BF)
        g_copy(i, p).start()

    def pre_grad_of(i, from_above):
        total = z[0, i].astype(F32) + z[1, i].astype(F32)
        if from_above:
            total = total + q[i].astype(F32)
        return (unpacked(total) * slope[chunk_of(i)]).astype(BF)

    def own_term(pre_grad):
        own[...] = dot(pre_grad, wu[...])

    def send_q(i, pre_grad):
        qsend[i] = packed(dot(pre_grad, near[...]))
        q_copy(i).start()

    def send_near_sum(i, near_sum):
        zn[i] = packed(near_sum)
        for k in range(2):
            zn_copy(i, k).start()

    def send_near(i):
        send_near_sum(i, dot_t(g[chunk_of(i)], wd1[...]))

    @pl.when(s == top)
    def _():
        def first(i, _):
            own_term(pre_grad_of(i, False))
            for p in range(PIECES):
                add_own(i, p, cot[chunk_of(i), cols(p)])
            return 0

        for k in range(GROUPS):
            base_from[k].wait_recv()
            lax.fori_loop(k * GROUP // CHUNK, (k + 1) * GROUP // CHUNK, first, 0)
        for k in range(GROUPS):
            base_copy[k].wait_send()
        g[...] = cot[...]

    def own_base(i):
        base = jnp.zeros((CHUNK, BAND), F32)
        for p in range(PIECES):
            g_copy(i, p).wait_recv()
            base = base + dot_t(g[chunk_of(i), cols(p)], wd[:, cols(p)])
        part_sum = packed(base)
        za[i] = part_sum
        za_copy(i).start()
        z[t, i] = part_sum

    def second(i):
        remote(za.at[i], z.at[other, i], za_s.at[i], z_r.at[i, other], s, other).wait_recv()
        pre_grad = pre_grad_of(i, False)
        own_term(pre_grad)
        for p in range(PIECES):
            add_own(i, p, g[chunk_of(i), cols(p)])
        return pre_grad

    @pl.when(s == top - 1)
    def _():
        own_base(0)
        own_base(1)

    coupling = jnp.zeros((BAND, BAND), F32)
    for p in range(PARTS):
        up1[p].wait_recv()
        up2[p].start()
        coupling = coupling + dot_t(wu[:, part(p)], wd1[:, part(p)])
    m1s[...] = coupling.astype(BF)
    m1_copy = remote(m1s, m1.at[t], m1_s, m1_r, s, other)
    m1_copy.start()

    @pl.when(s == top - 1)
    def _():
        send_near(0)
        send_near(1)

    @pl.when(takes_dn)
    def _():
        dn.wait_recv()
        m2s[...] = dot_t(wu1[...], wd1[...]).astype(BF)

    @pl.when(jnp.logical_not(takes_dn))
    def _():
        m2s[...] = jnp.zeros_like(m2s)

    m2_copy = [remote(m2s, m2.at[t], m2_s.at[k], m2_r.at[t], sec(1), k) for k in range(2)]
    m2_from = [remote(m2s, m2.at[k], m2_s.at[k], m2_r.at[k], sec(1), k) for k in range(2)]
    for copy in m2_copy:
        copy.start()

    @pl.when(s == top - 1)
    def _():
        kept[...] = second(0)
        own_base(2)
        send_near(2)

    m1_copy.wait_recv()
    near[...] = (m1s[...].astype(F32) + m1[other].astype(F32)).astype(BF)

    @pl.when(s == top - 1)
    def _():
        send_q(0, kept[...])

        def rest(i, _):
            send_q(i, second(i))

            @pl.when(i < CHUNKS - 2)
            def _():
                own_base(i + 2)
                send_near(i + 2)

            return 0

        lax.fori_loop(1, CHUNKS, rest, 0)

    for copy in m2_from:
        copy.wait_recv()
    far[...] = (0.5 * (m2[0].astype(F32) + m2[1].astype(F32))).astype(BF)

    sends_q = jnp.logical_and(s >= 2, s <= top - 1)
    sends_near = jnp.logical_or(s == top - 1, s == top - 2)
    sends_far = jnp.logical_and(s >= 3, s <= top - 2)

    def send_far(i, ahead):
        zf[i] = packed(ahead)
        for k in range(2):
            zf_copy(i, k).start()

    def arrive(i):
        z_from(i, 0).wait_recv()
        z_from(i, 1).wait_recv()
        q_copy(i).wait_recv()
        return pre_grad_of(i, True)

    @pl.when(s == top - 2)
    def _():
        def third(i, _):
            pre_grad = arrive(i)
            send_q(i, pre_grad)
            own_term(pre_grad)
            near_sum = jnp.zeros((CHUNK, BAND), F32)
            for p in range(PIECES):
                g_copy(i, p).wait_recv()
                entering = g[chunk_of(i), cols(p)]
                if p < PIECES - 1:
                    add_own(i, p, entering)
                near_sum = near_sum + dot_t(entering, wd1[:, cols(p)])
            send_near_sum(i, near_sum)
            add_own(i, PIECES - 1, entering)

            @pl.when(i == 0)
            def _():
                for p in range(PARTS):
                    up2[p].wait_recv()

            send_far(i, dot(pre_grad, far[...]) + dot_t(g[chunk_of(i)], wd2[...]))
            return 0

        lax.fori_loop(0, CHUNKS, third, 0)

    @pl.when(jnp.logical_and(s >= 1, s <= top - 3))
    def _():
        for p in range(PARTS):
            up2[p].wait_recv()

        def relay(i, _):
            pre_grad = arrive(i)

            @pl.when(s >= 2)
            def _():
                send_q(i, pre_grad)

            own_term(pre_grad)
            ahead = dot(pre_grad, far[...])
            for p in range(PIECES):
                g_copy(i, p).wait_recv()
                entering = g[chunk_of(i), cols(p)]
                if p < PIECES - 1:
                    add_own(i, p, entering)
                ahead = ahead + dot_t(entering, wd2[:, cols(p)])

            @pl.when(s >= 3)
            def _():
                send_far(i, ahead)

            add_own(i, PIECES - 1, entering)
            return 0

        lax.fori_loop(0, CHUNKS, relay, 0)

    @pl.when(s == 0)
    def _():
        def last(i, _):
            for p in range(PIECES):
                g_copy(i, p).wait_recv()
            return 0

        lax.fori_loop(0, CHUNKS, last, 0)

    loads[4].wait()
    row_basis, row_basis_t, pair_basis = row_ref[...], row_t_ref[...], pair_ref[...]
    grad = lax.dot_general(
        hidden[...], g[...], (((0,), (0,)), ((), ())), preferred_element_type=F32
    )
    moment = acc[...] + grad
    half = dot(row_basis, moment, HIGH)
    acc[...] = grad
    stacked = jnp.concatenate(
        [half[:, k * 2 * SPAN : (k + 1) * 2 * SPAN] for k in range(COLS // (2 * SPAN))], axis=0
    )
    coeffs = dot(stacked, pair_basis, HIGH)
    coef[...] = coeffs

    def share(k):
        return pl.ds(pl.multiple_of(k * SHARE, SHARE), SHARE)

    def c_copy(d):
        to = lax.rem(r + d, REPLICAS)
        return pltpu.make_async_remote_copy(
            coef.at[share(to)], heard.at[d], c_s.at[d], c_r.at[d],
            device_id=(to, s, t), device_id_type=MESH,
        )

    for d in range(1, REPLICAS):
        c_copy(d).start()
    heard[0] = coef[share(r)]

    synced = flag_ref[0] == 1
    back = dot_t(coeffs, pair_basis, HIGH)
    wide = jnp.concatenate(
        [back[k * LOW : (k + 1) * LOW] for k in range(COLS // (2 * SPAN))], axis=1
    )
    decoded = dot(row_basis_t, wide, HIGH)
    delta_ref[...] = jnp.where(synced, acc[...] - decoded, acc[...])

    for p in range(PARTS):
        up1[p].wait_send()
        up2[p].wait_send()

    @pl.when(sends_dn)
    def _():
        dn.wait_send()

    m1_copy.wait_send()
    for copy in m2_copy:
        copy.wait_send()

    @pl.when(jnp.logical_not(sends_far))
    def _():
        @pl.when(jnp.logical_not(jnp.logical_and(s >= 1, s <= top - 2)))
        def _():
            for p in range(PARTS):
                up2[p].wait_recv()

    def drain(i, _):
        @pl.when(s == top - 1)
        def _():
            za_copy(i).wait_send()

        @pl.when(sends_near)
        def _():
            for k in range(2):
                zn_copy(i, k).wait_send()

        @pl.when(sends_far)
        def _():
            for k in range(2):
                zf_copy(i, k).wait_send()

        @pl.when(sends_q)
        def _():
            q_copy(i).wait_send()

        @pl.when(s >= 1)
        def _():
            for p in range(PIECES):
                g_copy(i, p).wait_send()

        return 0

    lax.fori_loop(0, CHUNKS, drain, 0)

    for d in range(1, REPLICAS):
        c_copy(d).wait_recv()
    summed = heard[0]
    for d in range(1, REPLICAS):
        summed = summed + heard[d]
    mean = summed * (1.0 / REPLICAS)
    back = dot_t(mean, pair_basis, HIGH)
    wide = jnp.concatenate([back[k * LOW : (k + 1) * LOW] for k in range(SHARE // LOW)], axis=1)
    change_ref[...] = dot(row_basis_t, wide, HIGH)
    for d in range(1, REPLICAS):
        c_copy(d).wait_send()


def local(
    cotangent, saved_pre, up_band, down_band, accumulated, outer_momentum, band_freqs, sync_flags
):
    vmem = pl.BlockSpec(memory_space=pltpu.VMEM)
    hbm = pl.BlockSpec(memory_space=pltpu.HBM)
    share = COLS // REPLICAS
    dma = pltpu.SemaphoreType.DMA
    delta, change = pl.pallas_call(
        kernel,
        out_shape=(
            jax.ShapeDtypeStruct((BAND, COLS), F32),
            jax.ShapeDtypeStruct((BAND, share), F32),
        ),
        in_specs=[hbm] * 7,
        out_specs=(vmem, vmem),
        scratch_shapes=[
            pltpu.SMEM((2, LOW), jnp.int32),
            pltpu.SMEM((1,), jnp.int32),
            pltpu.VMEM((LOW, SPAN), F32),
            pltpu.VMEM((SPAN, LOW), F32),
            pltpu.VMEM((2 * SPAN, 2 * SPAN), F32),
            pltpu.VMEM((ROWS, COLS), BF),
            pltpu.VMEM((ROWS, BAND), BF),
            pltpu.VMEM((BAND, COLS), BF),
            pltpu.VMEM((BAND, COLS), BF),
            pltpu.VMEM((BAND, COLS), F32),
            pltpu.VMEM((ROWS, COLS), BF),
            pltpu.VMEM((ROWS, COLS), BF),
            pltpu.VMEM((BAND, COLS), BF),
            pltpu.VMEM((BAND, COLS), BF),
            pltpu.VMEM((BAND, COLS), BF),
            pltpu.VMEM((2, CHUNKS, HALF, 2 * BAND), BF),
            pltpu.VMEM((CHUNKS, HALF, 2 * BAND), BF),
            pltpu.VMEM((CHUNKS, HALF, 2 * BAND), BF),
            pltpu.VMEM((CHUNKS, HALF, 2 * BAND), BF),
            pltpu.VMEM((CHUNKS, HALF, 2 * BAND), BF),
            pltpu.VMEM((CHUNKS, HALF, 2 * BAND), BF),
            pltpu.VMEM((2, BAND, BAND), BF),
            pltpu.VMEM((2, BAND, BAND), BF),
            pltpu.VMEM((BAND, BAND), BF),
            pltpu.VMEM((BAND, BAND), BF),
            pltpu.VMEM((BAND, BAND), BF),
            pltpu.VMEM((BAND, BAND), BF),
            pltpu.VMEM((ROWS, BAND), F32),
            pltpu.VMEM((ROWS, BAND), BF),
            pltpu.VMEM((CHUNK, COLS), F32),
            pltpu.VMEM((CHUNK, BAND), BF),
            pltpu.VMEM((REPLICAS * SHARE, 2 * SPAN), F32),
            pltpu.VMEM((REPLICAS, SHARE, 2 * SPAN), F32),
            dma((7,)),
            dma((PARTS,)), dma((PARTS,)), dma((PARTS,)), dma((PARTS,)),
            dma, dma, dma, dma,
            dma((2,)), dma((2,)),
            dma((GROUPS,)), dma((GROUPS,)),
            dma((CHUNKS,)), dma((CHUNKS, 2)), dma((CHUNKS, 2)), dma((CHUNKS, 2)),
            dma((CHUNKS,)), dma((CHUNKS,)),
            dma((CHUNKS, PIECES)), dma((CHUNKS, PIECES)),
            dma((REPLICAS,)), dma((REPLICAS,)),
        ],
        compiler_params=pltpu.CompilerParams(
            collective_id=0, has_side_effects=True, vmem_limit_bytes=LIMIT << 20
        ),
        name="relay",
    )(
        band_freqs,
        sync_flags,
        cotangent.reshape(ROWS, COLS),
        saved_pre.reshape(ROWS, BAND),
        up_band[0],
        down_band[0],
        accumulated[0],
    )
    residual = accumulated + delta[None]
    synced = sync_flags[0] == 1
    prior = outer_momentum[0, 0]
    moved = momentum_decay * prior + change
    stepped = -outer_rate * (change + momentum_decay * moved)
    new_outer = jnp.where(synced, moved, prior)
    outer_step = jnp.where(synced, stepped, jnp.zeros_like(stepped))
    return (residual, new_outer[None, None], outer_step[None, None])


def solution(mesh):
    return jax.shard_map(
        local,
        mesh=mesh,
        in_specs=(
            P("replica", None, None, "tensor"),
            P("replica", "section", None, None, None),
            P("replica", "section", "tensor"),
            P("replica", "section", "tensor"),
            P("replica", "section", "tensor"),
            P("section", "tensor", None, "replica"),
            P(),
            P("section"),
        ),
        out_specs=(
            P("replica", "section", "tensor"),
            P("section", "tensor", None, "replica"),
            P("section", "tensor", None, "replica"),
        ),
        check_vma=False,
    )
```

```python
import math

import jax
import jax.numpy as jnp
from jax import lax
from jax.experimental import pallas as pl
from jax.experimental.pallas import tpu as pltpu
from jax.sharding import PartitionSpec as P

SPAN = 64
LOW = 8
momentum_decay = 0.9
outer_rate = 0.7

SECTIONS = 16
REPLICAS = 16
BAND = 64
COLS = 4096
ROWS = 192
CHUNK = 16
CHUNKS = ROWS // CHUNK
SHARE = COLS // (2 * SPAN) * LOW // REPLICAS
PIECES = 4
LIMIT = 60
GROUPS = 3
GROUP = ROWS // GROUPS
WIDTH = COLS // PIECES
PARTS = 4
PART = COLS // PARTS
HALF = CHUNK // 2
MESH = pl.DeviceIdType.MESH
HIGH = lax.Precision.HIGHEST
BF = jnp.bfloat16
F32 = jnp.float32


def dot(a, b, precision=None):
    return jnp.dot(a, b, preferred_element_type=F32, precision=precision)


def dot_t(a, b, precision=None):
    return lax.dot_general(
        a, b, (((1,), (1,)), ((), ())), preferred_element_type=F32, precision=precision
    )


def basis(freqs, position):
    turns = (freqs * (2 * position + 1)) & (4 * SPAN - 1)
    weight = jnp.where(freqs == 0, math.sqrt(1.0 / SPAN), math.sqrt(2.0 / SPAN))
    return weight * jnp.cos(turns.astype(F32) * (math.pi / (2 * SPAN)))


def freqs_along(freq_ref, row, which):
    out = jnp.zeros_like(which)
    for k in range(LOW):
        out = jnp.where(which == k, freq_ref[row, k], out)
    return out


def packed(block):
    return jnp.concatenate([block[:HALF], block[HALF:]], axis=1).astype(BF)


def unpacked(block):
    return jnp.concatenate([block[:, :BAND], block[:, BAND:]], axis=0)


def kernel(
    freq_hbm, flag_hbm, cot_hbm, pre_hbm, up_hbm, down_hbm, acc_hbm,
    delta_ref, change_ref,
    freq_ref, flag_ref, row_ref, row_t_ref, pair_ref,
    cot, pre_ref, wu, wd, acc, g, out, wd1, wd2, wu1, z, za, zn, zf, q, qsend, m1, m2, m1s, m2s, near, far,
    slope, hidden, own, kept, coef, heard,
    load_sem, up1_s, up1_r, up2_s, up2_r, dn_s, dn_r, m1_s, m1_r, m2_s, m2_r, zb_s, zb_r,
    za_s, zn_s, zf_s, z_r, q_s, q_r, g_s, g_r, c_s, c_r,
):
    r = lax.axis_index("replica")
    s = lax.axis_index("section")
    t = lax.axis_index("tensor")
    other = 1 - t
    top = SECTIONS - 1

    def sec(offset):
        return lax.rem(s + offset + SECTIONS, SECTIONS)

    def remote(src, dst, send, recv, section, tensor):
        return pltpu.make_async_remote_copy(
            src, dst, send, recv, device_id=(r, section, tensor), device_id_type=MESH
        )

    loads = [
        pltpu.make_async_copy(src, dst, load_sem.at[k])
        for k, (src, dst) in enumerate(
            (
                (pre_hbm, pre_ref),
                (down_hbm, wd),
                (cot_hbm, cot),
                (up_hbm, wu),
                (acc_hbm, acc),
                (freq_hbm, freq_ref),
                (flag_hbm, flag_ref),
            )
        )
    ]
    barrier = pltpu.get_barrier_semaphore()
    for offset in (-2, -1, 1, 2):
        for tensor in range(2):
            pl.semaphore_signal(
                barrier, inc=1, device_id=(r, sec(offset), tensor), device_id_type=MESH
            )
    pl.semaphore_signal(barrier, inc=1, device_id=(r, s, other), device_id_type=MESH)
    for d in range(1, REPLICAS):
        pl.semaphore_signal(
            barrier, inc=1, device_id=(lax.rem(r + d, REPLICAS), s, t), device_id_type=MESH
        )
    for load in loads:
        load.start()
    pl.semaphore_wait(barrier, 9 + REPLICAS - 1)

    def part(p):
        return pl.ds(p * PART, PART)

    up1 = [
        remote(down_hbm.at[:, part(p)], wd1.at[:, part(p)], up1_s.at[p], up1_r.at[p], sec(1), t)
        for p in range(PARTS)
    ]
    up2 = [
        remote(wd1.at[:, part(p)], wd2.at[:, part(p)], up2_s.at[p], up2_r.at[p], sec(1), t)
        for p in range(PARTS)
    ]
    dn = remote(up_hbm, wu1, dn_s, dn_r, sec(-1), t)
    for copy in up1:
        copy.start()

    sends_dn = s <= top - 2
    takes_dn = jnp.logical_or(s <= top - 3, s == top)

    @pl.when(sends_dn)
    def _():
        dn.start()

    for load in loads[:4]:
        load.wait()

    def base_rows(k):
        return pl.ds(k * (GROUP // CHUNK), GROUP // CHUNK)

    base_copy = [
        remote(za.at[base_rows(k)], z.at[t, base_rows(k)], zb_s.at[k], zb_r.at[k], s, other)
        for k in range(GROUPS)
    ]
    base_from = [
        remote(za.at[base_rows(k)], z.at[other, base_rows(k)], zb_s.at[k], zb_r.at[k], s, other)
        for k in range(GROUPS)
    ]

    @pl.when(s == top)
    def _():
        for k in range(GROUPS):
            base = dot_t(cot[pl.ds(k * GROUP, GROUP)], wd[...])
            for i in range(GROUP // CHUNK):
                za[k * (GROUP // CHUNK) + i] = packed(base[i * CHUNK : (i + 1) * CHUNK])
            base_copy[k].start()
            z[t, base_rows(k)] = za[base_rows(k)]

    pre = pre_ref[...].astype(F32)
    sigma = jax.nn.sigmoid(pre)
    slope[...] = sigma * (1.0 + pre * (1.0 - sigma))
    hidden[...] = (pre * sigma).astype(BF)

    for load in loads[5:]:
        load.wait()
    u_of = lax.broadcasted_iota(jnp.int32, (LOW, SPAN), 0)
    n_of = lax.broadcasted_iota(jnp.int32, (LOW, SPAN), 1)
    row_ref[...] = basis(freqs_along(freq_ref, 0, u_of), n_of)
    u_t = lax.broadcasted_iota(jnp.int32, (SPAN, LOW), 1)
    n_t = lax.broadcasted_iota(jnp.int32, (SPAN, LOW), 0)
    row_t_ref[...] = basis(freqs_along(freq_ref, 0, u_t), n_t)
    at_row = lax.broadcasted_iota(jnp.int32, (2 * SPAN, 2 * SPAN), 0)
    at_col = lax.broadcasted_iota(jnp.int32, (2 * SPAN, 2 * SPAN), 1)
    pair_ref[...] = jnp.where(
        at_col // LOW == at_row // SPAN,
        basis(freqs_along(freq_ref, 1, lax.rem(at_col, LOW)), lax.rem(at_row, SPAN)),
        0.0,
    )

    def cols(p):
        return pl.ds(p * WIDTH, WIDTH)

    def chunk_of(i):
        return pl.ds(pl.multiple_of(i * CHUNK, CHUNK), CHUNK)

    def q_copy(i):
        return remote(qsend.at[i], q.at[i], q_s.at[i], q_r.at[i], sec(-1), t)

    def za_copy(i):
        return remote(za.at[i], z.at[t, i], za_s.at[i], z_r.at[i, t], s, other)

    def zn_copy(i, k):
        return remote(zn.at[i], z.at[t, i], zn_s.at[i, k], z_r.at[i, t], sec(-1), k)

    def zf_copy(i, k):
        return remote(zf.at[i], z.at[t, i], zf_s.at[i, k], z_r.at[i, t], sec(-2), k)

    def z_from(i, k):
        return remote(zf.at[i], z.at[k, i], zf_s.at[i, k], z_r.at[i, k], sec(-2), k)

    def g_copy(i, p):
        at = (chunk_of(i), cols(p))
        return remote(out.at[at], g.at[at], g_s.at[i, p], g_r.at[i, p], sec(-1), t)

    def add_own(i, p, entering):
        passed = entering.astype(F32) + own[:, cols(p)]
        out[chunk_of(i), cols(p)] = passed.astype(BF)
        g_copy(i, p).start()

    def pre_grad_of(i, from_above):
        total = z[0, i].astype(F32) + z[1, i].astype(F32)
        if from_above:
            total = total + q[i].astype(F32)
        return (unpacked(total) * slope[chunk_of(i)]).astype(BF)

    def own_term(pre_grad):
        own[...] = dot(pre_grad, wu[...])

    def send_q(i, pre_grad):
        qsend[i] = packed(dot(pre_grad, near[...]))
        q_copy(i).start()

    def send_near_sum(i, near_sum):
        zn[i] = packed(near_sum)
        for k in (other, t):
            zn_copy(i, k).start()

    def send_near(i):
        send_near_sum(i, dot_t(g[chunk_of(i)], wd1[...]))

    @pl.when(s == top)
    def _():
        def first(i, _):
            own_term(pre_grad_of(i, False))
            for p in range(PIECES):
                add_own(i, p, cot[chunk_of(i), cols(p)])
            return 0

        for k in range(GROUPS):
            base_from[k].wait_recv()
            lax.fori_loop(k * GROUP // CHUNK, (k + 1) * GROUP // CHUNK, first, 0)
        for k in range(GROUPS):
            base_copy[k].wait_send()
        g[...] = cot[...]

    def own_base(i):
        base = jnp.zeros((CHUNK, BAND), F32)
        for p in range(PIECES):
            g_copy(i, p).wait_recv()
            base = base + dot_t(g[chunk_of(i), cols(p)], wd[:, cols(p)])
        part_sum = packed(base)
        za[i] = part_sum
        za_copy(i).start()
        z[t, i] = part_sum

    def second(i):
        remote(za.at[i], z.at[other, i], za_s.at[i], z_r.at[i, other], s, other).wait_recv()
        pre_grad = pre_grad_of(i, False)
        own_term(pre_grad)
        for p in range(PIECES):
            add_own(i, p, g[chunk_of(i), cols(p)])
        return pre_grad

    @pl.when(s == top - 1)
    def _():
        own_base(0)
        own_base(1)

    coupling = jnp.zeros((BAND, BAND), F32)
    for p in range(PARTS):
        up1[p].wait_recv()
        up2[p].start()
        coupling = coupling + dot_t(wu[:, part(p)], wd1[:, part(p)])
    m1s[...] = coupling.astype(BF)
    m1_copy = remote(m1s, m1.at[t], m1_s, m1_r, s, other)
    m1_copy.start()

    @pl.when(s == top - 1)
    def _():
        send_near(0)
        send_near(1)

    @pl.when(takes_dn)
    def _():
        dn.wait_recv()
        m2s[...] = dot_t(wu1[...], wd1[...]).astype(BF)

    @pl.when(jnp.logical_not(takes_dn))
    def _():
        m2s[...] = jnp.zeros_like(m2s)

    m2_copy = [remote(m2s, m2.at[t], m2_s.at[k], m2_r.at[t], sec(1), k) for k in range(2)]
    m2_from = [remote(m2s, m2.at[k], m2_s.at[k], m2_r.at[k], sec(1), k) for k in range(2)]
    for copy in m2_copy:
        copy.start()

    @pl.when(s == top - 1)
    def _():
        kept[...] = second(0)
        own_base(2)
        send_near(2)

    m1_copy.wait_recv()
    near[...] = (m1s[...].astype(F32) + m1[other].astype(F32)).astype(BF)

    @pl.when(s == top - 1)
    def _():
        send_q(0, kept[...])

        def rest(i, _):
            send_q(i, second(i))

            @pl.when(i < CHUNKS - 2)
            def _():
                own_base(i + 2)
                send_near(i + 2)

            return 0

        lax.fori_loop(1, CHUNKS, rest, 0)

    for copy in m2_from:
        copy.wait_recv()
    far[...] = (0.5 * (m2[0].astype(F32) + m2[1].astype(F32))).astype(BF)

    sends_q = jnp.logical_and(s >= 2, s <= top - 1)
    sends_near = jnp.logical_or(s == top - 1, s == top - 2)
    sends_far = jnp.logical_and(s >= 3, s <= top - 2)

    def send_far(i, ahead):
        zf[i] = packed(ahead)
        for k in (other, t):
            zf_copy(i, k).start()

    def arrive(i):
        z_from(i, 0).wait_recv()
        z_from(i, 1).wait_recv()
        q_copy(i).wait_recv()
        return pre_grad_of(i, True)

    @pl.when(s == top - 2)
    def _():
        def third(i, _):
            pre_grad = arrive(i)
            send_q(i, pre_grad)
            own_term(pre_grad)
            near_sum = jnp.zeros((CHUNK, BAND), F32)
            for p in range(PIECES):
                g_copy(i, p).wait_recv()
                entering = g[chunk_of(i), cols(p)]
                if p < PIECES - 1:
                    add_own(i, p, entering)
                near_sum = near_sum + dot_t(entering, wd1[:, cols(p)])
            send_near_sum(i, near_sum)
            add_own(i, PIECES - 1, entering)

            @pl.when(i == 0)
            def _():
                for p in range(PARTS):
                    up2[p].wait_recv()

            send_far(i, dot(pre_grad, far[...]) + dot_t(g[chunk_of(i)], wd2[...]))
            return 0

        lax.fori_loop(0, CHUNKS, third, 0)

    @pl.when(jnp.logical_and(s >= 1, s <= top - 3))
    def _():
        for p in range(PARTS):
            up2[p].wait_recv()

        def relay(i, _):
            pre_grad = arrive(i)

            @pl.when(s >= 2)
            def _():
                send_q(i, pre_grad)

            own_term(pre_grad)
            ahead = dot(pre_grad, far[...])
            for p in range(PIECES):
                g_copy(i, p).wait_recv()
                entering = g[chunk_of(i), cols(p)]
                if p < PIECES - 1:
                    add_own(i, p, entering)
                ahead = ahead + dot_t(entering, wd2[:, cols(p)])

            @pl.when(s >= 3)
            def _():
                send_far(i, ahead)

            add_own(i, PIECES - 1, entering)
            return 0

        lax.fori_loop(0, CHUNKS, relay, 0)

    @pl.when(s == 0)
    def _():
        def last(i, _):
            for p in range(PIECES):
                g_copy(i, p).wait_recv()
            return 0

        lax.fori_loop(0, CHUNKS, last, 0)

    loads[4].wait()
    row_basis, row_basis_t, pair_basis = row_ref[...], row_t_ref[...], pair_ref[...]
    grad = lax.dot_general(
        hidden[...], g[...], (((0,), (0,)), ((), ())), preferred_element_type=F32
    )
    moment = acc[...] + grad
    half = dot(row_basis, moment, HIGH)
    acc[...] = grad
    stacked = jnp.concatenate(
        [half[:, k * 2 * SPAN : (k + 1) * 2 * SPAN] for k in range(COLS // (2 * SPAN))], axis=0
    )
    coeffs = dot(stacked, pair_basis, HIGH)
    coef[...] = coeffs

    def share(k):
        return pl.ds(pl.multiple_of(k * SHARE, SHARE), SHARE)

    def c_copy(d):
        to = lax.rem(r + d, REPLICAS)
        return pltpu.make_async_remote_copy(
            coef.at[share(to)], heard.at[d], c_s.at[d], c_r.at[d],
            device_id=(to, s, t), device_id_type=MESH,
        )

    for d in range(1, REPLICAS):
        c_copy(d).start()
    heard[0] = coef[share(r)]

    synced = flag_ref[0] == 1
    back = dot_t(coeffs, pair_basis, HIGH)
    wide = jnp.concatenate(
        [back[k * LOW : (k + 1) * LOW] for k in range(COLS // (2 * SPAN))], axis=1
    )
    decoded = dot(row_basis_t, wide, HIGH)
    delta_ref[...] = jnp.where(synced, acc[...] - decoded, acc[...])

    for p in range(PARTS):
        up1[p].wait_send()
        up2[p].wait_send()

    @pl.when(sends_dn)
    def _():
        dn.wait_send()

    m1_copy.wait_send()
    for copy in m2_copy:
        copy.wait_send()

    @pl.when(jnp.logical_not(sends_far))
    def _():
        @pl.when(jnp.logical_not(jnp.logical_and(s >= 1, s <= top - 2)))
        def _():
            for p in range(PARTS):
                up2[p].wait_recv()

    def drain(i, _):
        @pl.when(s == top - 1)
        def _():
            za_copy(i).wait_send()

        @pl.when(sends_near)
        def _():
            for k in range(2):
                zn_copy(i, k).wait_send()

        @pl.when(sends_far)
        def _():
            for k in range(2):
                zf_copy(i, k).wait_send()

        @pl.when(sends_q)
        def _():
            q_copy(i).wait_send()

        @pl.when(s >= 1)
        def _():
            for p in range(PIECES):
                g_copy(i, p).wait_send()

        return 0

    lax.fori_loop(0, CHUNKS, drain, 0)

    for d in range(1, REPLICAS):
        c_copy(d).wait_recv()
    summed = heard[0]
    for d in range(1, REPLICAS):
        summed = summed + heard[d]
    mean = summed * (1.0 / REPLICAS)
    back = dot_t(mean, pair_basis, HIGH)
    wide = jnp.concatenate([back[k * LOW : (k + 1) * LOW] for k in range(SHARE // LOW)], axis=1)
    change_ref[...] = dot(row_basis_t, wide, HIGH)
    for d in range(1, REPLICAS):
        c_copy(d).wait_send()


def local(
    cotangent, saved_pre, up_band, down_band, accumulated, outer_momentum, band_freqs, sync_flags
):
    vmem = pl.BlockSpec(memory_space=pltpu.VMEM)
    hbm = pl.BlockSpec(memory_space=pltpu.HBM)
    share = COLS // REPLICAS
    dma = pltpu.SemaphoreType.DMA
    delta, change = pl.pallas_call(
        kernel,
        out_shape=(
            jax.ShapeDtypeStruct((BAND, COLS), F32),
            jax.ShapeDtypeStruct((BAND, share), F32),
        ),
        in_specs=[hbm] * 7,
        out_specs=(vmem, vmem),
        scratch_shapes=[
            pltpu.SMEM((2, LOW), jnp.int32),
            pltpu.SMEM((1,), jnp.int32),
            pltpu.VMEM((LOW, SPAN), F32),
            pltpu.VMEM((SPAN, LOW), F32),
            pltpu.VMEM((2 * SPAN, 2 * SPAN), F32),
            pltpu.VMEM((ROWS, COLS), BF),
            pltpu.VMEM((ROWS, BAND), BF),
            pltpu.VMEM((BAND, COLS), BF),
            pltpu.VMEM((BAND, COLS), BF),
            pltpu.VMEM((BAND, COLS), F32),
            pltpu.VMEM((ROWS, COLS), BF),
            pltpu.VMEM((ROWS, COLS), BF),
            pltpu.VMEM((BAND, COLS), BF),
            pltpu.VMEM((BAND, COLS), BF),
            pltpu.VMEM((BAND, COLS), BF),
            pltpu.VMEM((2, CHUNKS, HALF, 2 * BAND), BF),
            pltpu.VMEM((CHUNKS, HALF, 2 * BAND), BF),
            pltpu.VMEM((CHUNKS, HALF, 2 * BAND), BF),
            pltpu.VMEM((CHUNKS, HALF, 2 * BAND), BF),
            pltpu.VMEM((CHUNKS, HALF, 2 * BAND), BF),
            pltpu.VMEM((CHUNKS, HALF, 2 * BAND), BF),
            pltpu.VMEM((2, BAND, BAND), BF),
            pltpu.VMEM((2, BAND, BAND), BF),
            pltpu.VMEM((BAND, BAND), BF),
            pltpu.VMEM((BAND, BAND), BF),
            pltpu.VMEM((BAND, BAND), BF),
            pltpu.VMEM((BAND, BAND), BF),
            pltpu.VMEM((ROWS, BAND), F32),
            pltpu.VMEM((ROWS, BAND), BF),
            pltpu.VMEM((CHUNK, COLS), F32),
            pltpu.VMEM((CHUNK, BAND), BF),
            pltpu.VMEM((REPLICAS * SHARE, 2 * SPAN), F32),
            pltpu.VMEM((REPLICAS, SHARE, 2 * SPAN), F32),
            dma((7,)),
            dma((PARTS,)), dma((PARTS,)), dma((PARTS,)), dma((PARTS,)),
            dma, dma, dma, dma,
            dma((2,)), dma((2,)),
            dma((GROUPS,)), dma((GROUPS,)),
            dma((CHUNKS,)), dma((CHUNKS, 2)), dma((CHUNKS, 2)), dma((CHUNKS, 2)),
            dma((CHUNKS,)), dma((CHUNKS,)),
            dma((CHUNKS, PIECES)), dma((CHUNKS, PIECES)),
            dma((REPLICAS,)), dma((REPLICAS,)),
        ],
        compiler_params=pltpu.CompilerParams(
            collective_id=0, has_side_effects=True, vmem_limit_bytes=LIMIT << 20
        ),
        name="relay",
    )(
        band_freqs,
        sync_flags,
        cotangent.reshape(ROWS, COLS),
        saved_pre.reshape(ROWS, BAND),
        up_band[0],
        down_band[0],
        accumulated[0],
    )
    residual = accumulated + delta[None]
    synced = sync_flags[0] == 1
    prior = outer_momentum[0, 0]
    moved = momentum_decay * prior + change
    stepped = -outer_rate * (change + momentum_decay * moved)
    new_outer = jnp.where(synced, moved, prior)
    outer_step = jnp.where(synced, stepped, jnp.zeros_like(stepped))
    return (residual, new_outer[None, None], outer_step[None, None])


def solution(mesh):
    return jax.shard_map(
        local,
        mesh=mesh,
        in_specs=(
            P("replica", None, None, "tensor"),
            P("replica", "section", None, None, None),
            P("replica", "section", "tensor"),
            P("replica", "section", "tensor"),
            P("replica", "section", "tensor"),
            P("section", "tensor", None, "replica"),
            P(),
            P("section"),
        ),
        out_specs=(
            P("replica", "section", "tensor"),
            P("section", "tensor", None, "replica"),
            P("section", "tensor", None, "replica"),
        ),
        check_vma=False,
    )
```
